512 devices in a mesh: dp: 32 (over x, z_lo, core), fsdp: 16 (over z_hi, y).
Axes of the slice: x: 4, y: 8, z: 8 (z_hi: 2, z_lo: 4; z = z_hi * 4 + z_lo), core: 2. Of those that a mesh axis runs over, the one named last changes fastest.
Arguments:
- hidden: bfloat16 [4096, 1536], P('dp', 'fsdp'), may hold values from -0.5 to 0.5
- teacher: bfloat16 [4096, 4096], P('dp', 'fsdp'), may hold values from -40 to 40
- projector: bfloat16 [1536, 1536], P('fsdp'), may hold values from -0.15625 to 0.15625
Outputs:
- grad_hidden: float32 [4096, 1536], P('dp', 'fsdp')
- grad_proj: float32 [1536, 1536], P('fsdp')
- loss: float32 [], replicated
The draws below stay inside these ranges and needn't reach their ends.
All inputs are finite; a program needn't handle non-finite values.
Results may differ from the reference program's by a relative error of at most 0.0085.
The reference program's roundings to bfloat16 on the way (of `student`, `target` and `grad_embed`) count: a program that leaves them out, or rounds other values in their place, can miss the bound.
Values may be sent and summed in bfloat16 or wider, within the bound.
No kernel may reach another device: no remote copies, remote signals or barrier semaphores. Data moves between devices by JAX's collectives and lax.ppermute only.
A program may use at most 64 MiB of HBM per device.

```python
import jax
import jax.numpy as jnp
from jax import lax

DS = 1536
DT = 4096
ROWS = 128
TEXTS = 4096


def draw_hidden(key, part):
    key_a = jax.random.fold_in(key, 11)
    key_b = jax.random.fold_in(key, 12)
    scales = jnp.exp(jax.random.uniform(key_b, (TEXTS, 1), jnp.float32, jnp.log(0.5), jnp.log(5.0)))
    values = jnp.clip(jax.random.normal(key_a, (TEXTS, DS), jnp.float32), -4.0, 4.0)
    return (0.025 * scales * values).astype(jnp.bfloat16)


def draw_teacher(key, part):
    key_a = jax.random.fold_in(key, 21)
    key_b = jax.random.fold_in(key, 22)
    scales = jnp.exp(jax.random.uniform(key_b, (TEXTS, 1), jnp.float32, 0.0, jnp.log(10.0)))
    values = jnp.clip(jax.random.normal(key_a, (TEXTS, DT), jnp.float32), -4.0, 4.0)
    return (scales * values).astype(jnp.bfloat16)


def block_scale(stream_key, shape, shards, least, largest):
    factor_of = 1.0
    for axis_at, shards_of in shards:
        steps = jax.random.uniform(jax.random.fold_in(jax.random.fold_in(stream_key, 6), axis_at), (shards_of,), jnp.float32, least / len(shards), largest / len(shards))
        factor_of = factor_of * jnp.repeat(jnp.exp(steps), shape[axis_at] // shards_of).reshape((-1,) + (1,) * (len(shape) - 1 - axis_at))
    return factor_of


def bell_draw(stream_key, shape, scale, most, pieces=(), held_as=jnp.bfloat16):
    array = scale * jax.random.normal(stream_key, shape, jnp.float32)
    if pieces:
        array = array * block_scale(stream_key, shape, pieces, -0.22, 0.18)
    return jnp.clip(array, -most, most).astype(held_as)


def setup_inputs(seed: int = 0) -> dict:
    seeds = jax.random.split(jax.random.key(seed), 4)
    return {
        "hidden": draw_hidden(jax.random.fold_in(seeds[3], 71), 0),
        "teacher": draw_teacher(jax.random.fold_in(seeds[3], 71), 0),
        "projector": bell_draw(seeds[2], (DS, DS), DS ** -0.5, 0.15625, ((0, 16),)),
    }


EPSILON = 1e-06

def reference(hidden, teacher, projector):
    embed = jnp.dot(hidden, projector, preferred_element_type=jnp.float32)
    inv_student = lax.rsqrt(lax.optimization_barrier(jnp.sum(embed * embed, axis=1, keepdims=True)) + EPSILON)
    unit_f = embed * inv_student
    student = unit_f.astype(jnp.bfloat16)
    student_f = student.astype(jnp.float32)
    teach_f = teacher.astype(jnp.float32)
    inv_teacher = lax.rsqrt(lax.optimization_barrier(jnp.sum(teach_f * teach_f, axis=1, keepdims=True)) + EPSILON)
    target = (teach_f * inv_teacher).astype(jnp.bfloat16)
    block_count = TEXTS // ROWS

    def one_block(index):
        begin = (index * ROWS).astype(jnp.int32)
        s_rows = lax.dynamic_slice_in_dim(student, begin, ROWS, 0)
        t_rows = lax.dynamic_slice_in_dim(target, begin, ROWS, 0)
        differ = jnp.dot(s_rows, student.T, preferred_element_type=jnp.float32) - jnp.dot(t_rows, target.T, preferred_element_type=jnp.float32)
        grad_rows = jnp.dot(differ, student_f, precision=lax.Precision.HIGHEST, preferred_element_type=jnp.float32)
        return (jnp.sum(differ * differ), 4.0 * grad_rows)
    sums, grads = lax.map(one_block, jnp.arange(block_count, dtype=jnp.int32))
    grad_unit = grads.reshape(TEXTS, DS)
    radial = lax.optimization_barrier(jnp.sum(unit_f * grad_unit, axis=1, keepdims=True))
    grad_embed = (inv_student * (grad_unit - unit_f * radial)).astype(jnp.bfloat16)
    grad_hidden = jnp.dot(grad_embed, projector.T, preferred_element_type=jnp.float32)
    grad_proj = jnp.dot(hidden.T, grad_embed, preferred_element_type=jnp.float32)
    loss = jnp.sum(sums) / TEXTS
    return (grad_hidden, grad_proj, loss)
```

```python
import jax
import jax.numpy as jnp
from jax import lax
from jax.sharding import Mesh
from jax.sharding import PartitionSpec as P

EPSILON = 1e-06
DP = ("x", "zl", "c")
FS = ("zh", "y")
XZ = ("x", "zl")
SIZES = {"x": 4, "zl": 4, "c": 2, "zh": 2, "y": 8}
SWAP = [(0, 1), (1, 0)]
ROWS_T = (((1,), (1,)), ((), ()))
COLS_T = (((0,), (0,)), ((), ()))


def dot(a, b, dims=(((1,), (0,)), ((), ()))):
    return lax.dot_general(a, b, dims, preferred_element_type=jnp.float32)


def group(axes):
    total = 1
    for axis in axes:
        total *= SIZES[axis]
    return total


def exchange(blocks, axes):
    return lax.all_to_all(blocks, axes, split_axis=0, concat_axis=0, tiled=True)


def gather(block, axes):
    copies = jnp.broadcast_to(block[None], (group(axes),) + block.shape)
    return exchange(copies, axes)


def pieces(value):
    high = lax.reduce_precision(value, 8, 7)
    rest = value - high
    middle = lax.reduce_precision(rest, 8, 7)
    low = rest - middle
    return [part.astype(jnp.bfloat16) for part in (high, middle, low)]


def body(hidden, teacher, projector):
    rows, width = hidden.shape
    full = projector.shape[1]
    group_fs, group_xz = group(FS), group(XZ)
    mine = rows // group_fs
    half = width // 2
    place = lax.axis_index(FS)
    core = lax.axis_index("c")

    teach = gather(teacher, FS).astype(jnp.float32)
    sq_teacher = jnp.sum(teach * teach, axis=(0, 2))
    target = (teach * lax.rsqrt(sq_teacher + EPSILON)[None, :, None]).astype(jnp.bfloat16)
    target = target.transpose(1, 0, 2).reshape(rows, -1)
    target_mine = lax.dynamic_slice_in_dim(target, place * mine, mine, 0)

    partial_embed = dot(hidden, projector).reshape(group_fs, mine, full)
    embed = jnp.sum(exchange(partial_embed, FS), axis=0)
    inv_student = lax.rsqrt(jnp.sum(embed * embed, axis=1, keepdims=True) + EPSILON)
    unit = embed * inv_student
    student = unit.astype(jnp.bfloat16)

    both = gather(jnp.concatenate([student, target_mine], axis=1), XZ).reshape(group_xz * mine, -1)
    s_rows, t_rows = both[:, :full], both[:, full:]
    s_here = gather(student, FS).reshape(rows, full)
    s_there = lax.ppermute(s_here, "c", SWAP)
    t_there = lax.ppermute(target, "c", SWAP)
    s_cols = jnp.concatenate([s_here, s_there], axis=0)
    t_cols = jnp.concatenate([target, t_there], axis=0)
    differ = dot(s_rows, s_cols, ROWS_T) - dot(t_rows, t_cols, ROWS_T)
    squares = jnp.sum(differ * differ)
    partial_grad = sum(dot(part, s_cols) for part in pieces(differ)[::-1])
    grad_unit = 4.0 * jnp.sum(
        exchange(partial_grad.reshape(group_xz, mine, full), XZ), axis=0
    )
    radial = jnp.sum(unit * grad_unit, axis=1, keepdims=True)
    grad_embed = (inv_student * (grad_unit - unit * radial)).astype(jnp.bfloat16)

    lane = lax.broadcasted_iota(jnp.int32, (mine, 128), 1)
    tail = jnp.zeros((mine, 128), jnp.bfloat16)
    for index, part in enumerate(pieces(squares)):
        tail = jnp.where(lane == index, part, tail)
    wide = gather(jnp.concatenate([grad_embed, tail], axis=1), FS).reshape(rows, -1)
    wide_there = lax.ppermute(wide, "c", SWAP)
    piece, piece_there = wide[:, :full], wide_there[:, :full]
    grad_hidden = dot(piece, projector, ROWS_T)

    hidden_there = lax.ppermute(hidden, "c", SWAP)
    left = lax.dynamic_slice_in_dim(hidden, core * half, half, 1)
    left_there = lax.dynamic_slice_in_dim(hidden_there, core * half, half, 1)
    proj_piece = dot(left, piece, COLS_T) + dot(left_there, piece_there, COLS_T)

    def loss_of(array):
        return jnp.sum(array.reshape(group_fs, mine, -1)[:, 0, full:].astype(jnp.float32))

    loss_part = loss_of(wide) + loss_of(wide_there)
    blocks = jnp.concatenate(
        [
            proj_piece.reshape(group_xz, half // group_xz, full),
            jnp.broadcast_to(loss_part, (group_xz, 1, full)),
        ],
        axis=1,
    )
    summed = jnp.sum(exchange(blocks, XZ), axis=0)
    loss = summed[-1, 0] / (rows * group(DP))
    grad_proj = lax.all_gather(
        gather(summed[:-1], XZ).reshape(half, full), "c", axis=0, tiled=True
    )
    return (grad_hidden, grad_proj, loss)


def solution(mesh):
    fine = Mesh(mesh.devices.reshape([SIZES[axis] for axis in DP + FS]), DP + FS)
    return jax.shard_map(
        body,
        mesh=fine,
        in_specs=(P(DP, FS), P(DP, FS), P(FS, None)),
        out_specs=(P(DP, FS), P(FS, None), P()),
        check_vma=False,
    )
```

```python
import jax
import jax.numpy as jnp
from jax import lax
from jax.sharding import Mesh
from jax.sharding import PartitionSpec as P

EPSILON = 1e-06
DP = ("x", "zl", "c")
FS = ("zh", "y")
XZ = ("x", "zl")
SIZES = {"x": 4, "zl": 4, "c": 2, "zh": 2, "y": 8}
SWAP = [(0, 1), (1, 0)]
ROWS_T = (((1,), (1,)), ((), ()))
COLS_T = (((0,), (0,)), ((), ()))


def dot(a, b, dims=(((1,), (0,)), ((), ()))):
    return lax.dot_general(a, b, dims, preferred_element_type=jnp.float32)


def group(axes):
    total = 1
    for axis in axes:
        total *= SIZES[axis]
    return total


def exchange(blocks, axes):
    return lax.all_to_all(blocks, axes, split_axis=0, concat_axis=0, tiled=True)


def gather(block, axes):
    copies = jnp.broadcast_to(block[None], (group(axes),) + block.shape)
    return exchange(copies, axes)


def pieces(value):
    high = lax.reduce_precision(value, 8, 7)
    rest = value - high
    middle = lax.reduce_precision(rest, 8, 7)
    low = rest - middle
    return [part.astype(jnp.bfloat16) for part in (high, middle, low)]


def body(hidden, teacher, projector):
    rows, width = hidden.shape
    full = projector.shape[1]
    group_fs, group_xz = group(FS), group(XZ)
    mine = rows // group_fs
    half = width // 2
    place = lax.axis_index(FS)
    core = lax.axis_index("c")

    teach_pair = jnp.concatenate([teacher, lax.ppermute(teacher, "zh", SWAP)], axis=1)
    teach = lax.all_gather(teach_pair, "y", axis=0).astype(jnp.float32)
    sq_teacher = jnp.sum(teach * teach, axis=(0, 2))
    target = (teach * lax.rsqrt(sq_teacher + EPSILON)[None, :, None]).astype(jnp.bfloat16)
    target = target.transpose(1, 0, 2).reshape(rows, -1)
    hidden_there = lax.ppermute(hidden, "c", SWAP)
    target, hidden_there = lax.optimization_barrier((target, hidden_there))
    target_mine = lax.dynamic_slice_in_dim(target, place * mine, mine, 0)

    partial_embed = dot(hidden, projector).reshape(group_fs, mine, full)
    embed = jnp.sum(exchange(partial_embed, FS), axis=0)
    inv_student = lax.rsqrt(jnp.sum(embed * embed, axis=1, keepdims=True) + EPSILON)
    unit = embed * inv_student
    student = unit.astype(jnp.bfloat16)

    both = gather(jnp.concatenate([student, target_mine], axis=1), XZ).reshape(group_xz * mine, -1)
    s_rows, t_rows = both[:, :full], both[:, full:]
    s_here = gather(student, FS).reshape(rows, full)
    s_there = lax.ppermute(s_here, "c", SWAP)
    t_there = lax.ppermute(target, "c", SWAP)
    s_cols = jnp.concatenate([s_here, s_there], axis=0)
    t_cols = jnp.concatenate([target, t_there], axis=0)
    differ = dot(s_rows, s_cols, ROWS_T) - dot(t_rows, t_cols, ROWS_T)
    squares = jnp.sum(differ * differ)
    squares = (squares + lax.ppermute(squares, "c", SWAP))
    partial_grad = sum(dot(part, s_cols) for part in pieces(differ)[::-1])
    grad_unit = 4.0 * jnp.sum(
        exchange(partial_grad.reshape(group_xz, mine, full), XZ), axis=0
    )
    radial = jnp.sum(unit * grad_unit, axis=1, keepdims=True)
    grad_embed = (inv_student * (grad_unit - unit * radial)).astype(jnp.bfloat16)

    lane = lax.broadcasted_iota(jnp.int32, (mine, 128), 1)
    tail = jnp.zeros((mine, 128), jnp.bfloat16)
    for index, part in enumerate(pieces(squares)):
        tail = jnp.where(lane == index, part, tail)
    wide = gather(jnp.concatenate([grad_embed, tail], axis=1), FS).reshape(rows, -1)
    piece = wide[:, :full]
    piece_there = lax.ppermute(piece, "c", SWAP)
    grad_hidden = dot(piece, projector, ROWS_T)

    left = lax.dynamic_slice_in_dim(hidden, core * half, half, 1)
    left_there = lax.dynamic_slice_in_dim(hidden_there, core * half, half, 1)
    proj_piece = dot(left, piece, COLS_T) + dot(left_there, piece_there, COLS_T)

    loss_part = jnp.sum(
        wide.reshape(group_fs, mine, -1)[:, 0, full:].astype(jnp.float32)
    )
    blocks = jnp.concatenate(
        [
            proj_piece.reshape(group_xz, half // group_xz, full),
            jnp.broadcast_to(loss_part, (group_xz, 1, full)),
        ],
        axis=1,
    )
    summed = jnp.sum(exchange(blocks, XZ), axis=0)
    loss = summed[-1, 0] / (rows * group(DP))
    grad_proj = lax.all_gather(
        gather(summed[:-1], XZ).reshape(half, full), "c", axis=0, tiled=True
    )
    return (grad_hidden, grad_proj, loss)


def solution(mesh):
    fine = Mesh(mesh.devices.reshape([SIZES[axis] for axis in DP + FS]), DP + FS)
    return jax.shard_map(
        body,
        mesh=fine,
        in_specs=(P(DP, FS), P(DP, FS), P(FS, None)),
        out_specs=(P(DP, FS), P(FS, None), P()),
        check_vma=False,
    )
```

```python
import jax
import jax.numpy as jnp
from jax import lax
from jax.sharding import Mesh
from jax.sharding import PartitionSpec as P

EPSILON = 1e-06
DP = ("x", "zl", "c")
FS = ("zh", "y")
XZ = ("x", "zl")
SIZES = {"x": 4, "zl": 4, "c": 2, "zh": 2, "y": 8}
SWAP = [(0, 1), (1, 0)]
ROWS_T = (((1,), (1,)), ((), ()))
COLS_T = (((0,), (0,)), ((), ()))


def dot(a, b, dims=(((1,), (0,)), ((), ()))):
    return lax.dot_general(a, b, dims, preferred_element_type=jnp.float32)


def group(axes):
    total = 1
    for axis in axes:
        total *= SIZES[axis]
    return total


def exchange(blocks, axes):
    return lax.all_to_all(blocks, axes, split_axis=0, concat_axis=0, tiled=True)


def gather(block, axes):
    copies = jnp.broadcast_to(block[None], (group(axes),) + block.shape)
    return exchange(copies, axes)


def pieces(value):
    high = lax.reduce_precision(value, 8, 7)
    rest = value - high
    middle = lax.reduce_precision(rest, 8, 7)
    low = rest - middle
    return [part.astype(jnp.bfloat16) for part in (high, middle, low)]


def normal(values, axes):
    total = jnp.sum(values * values, axis=axes, keepdims=True)
    return (values * lax.rsqrt(total + EPSILON)).astype(jnp.bfloat16)


def body(hidden, teacher, projector):
    rows, width = hidden.shape
    full = projector.shape[1]
    group_fs, group_xz = group(FS), group(XZ)
    mine = rows // group_fs
    half = width // 2
    width_t = teacher.shape[1]
    core = lax.axis_index("c")

    over = lax.ppermute(teacher, "zh", SWAP)
    first = lax.axis_index("zh") == 0
    pair = jnp.concatenate(
        [jnp.where(first, teacher, over), jnp.where(first, over, teacher)], axis=1
    )
    teach = lax.all_gather(pair, "y", axis=0).astype(jnp.float32)
    target = normal(teach, (0, 2)).transpose(1, 0, 2).reshape(rows, -1)

    partial_embed = dot(hidden, projector).astype(jnp.bfloat16)
    sent = jnp.concatenate(
        [
            partial_embed.reshape(group_fs, mine, full),
            teacher.reshape(group_fs, mine, width_t),
        ],
        axis=2,
    )
    got = exchange(sent, FS)
    embed = jnp.sum(got[:, :, :full].astype(jnp.float32), axis=0)
    inv_student = lax.rsqrt(jnp.sum(embed * embed, axis=1, keepdims=True) + EPSILON)
    unit = embed * inv_student
    student = unit.astype(jnp.bfloat16)
    target_mine = (
        normal(got[:, :, full:].astype(jnp.float32), (0, 2))
        .reshape(SIZES["zh"], SIZES["y"], mine, width_t)
        .transpose(2, 1, 0, 3)
        .reshape(mine, -1)
    )

    s_here = gather(student, FS).reshape(rows, full)
    both = gather(jnp.concatenate([student, target_mine], axis=1), ("zl",))
    both = gather(both.reshape(-1, both.shape[2]), ("x",)).reshape(group_xz * mine, -1)
    s_rows, t_rows = both[:, :full], both[:, full:]
    s_there = lax.ppermute(s_here, "c", SWAP)
    hidden_there = lax.ppermute(hidden, "c", SWAP)
    target, hidden_there = lax.optimization_barrier((target, hidden_there))
    t_there = lax.ppermute(target, "c", SWAP)
    s_cols = jnp.concatenate([s_here, s_there], axis=0)
    t_cols = jnp.concatenate([target, t_there], axis=0)
    differ = dot(s_rows, s_cols, ROWS_T) - dot(t_rows, t_cols, ROWS_T)
    squares = jnp.sum(differ * differ)
    squares = (squares + lax.ppermute(squares, "c", SWAP))
    partial_grad = sum(dot(part, s_cols) for part in pieces(differ)[::-1])
    partial_grad = partial_grad.astype(jnp.bfloat16).reshape(group_xz, mine, full)
    grad_unit = 4.0 * jnp.sum(exchange(partial_grad, XZ).astype(jnp.float32), axis=0)
    radial = jnp.sum(unit * grad_unit, axis=1, keepdims=True)
    grad_embed = (inv_student * (grad_unit - unit * radial)).astype(jnp.bfloat16)

    lane = lax.broadcasted_iota(jnp.int32, (mine, 128), 1)
    tail = jnp.zeros((mine, 128), jnp.bfloat16)
    for index, part in enumerate(pieces(squares)):
        tail = jnp.where(lane == index, part, tail)
    wide = gather(jnp.concatenate([grad_embed, tail], axis=1), FS).reshape(rows, -1)
    piece = wide[:, :full]
    piece_there = lax.ppermute(piece, "c", SWAP)
    grad_hidden = dot(piece, projector, ROWS_T)

    left = lax.dynamic_slice_in_dim(hidden, core * half, half, 1)
    left_there = lax.dynamic_slice_in_dim(hidden_there, core * half, half, 1)
    proj_piece = dot(left, piece, COLS_T) + dot(left_there, piece_there, COLS_T)

    loss_part = jnp.sum(
        wide.reshape(group_fs, mine, -1)[:, 0, full:].astype(jnp.float32)
    )
    blocks = jnp.concatenate(
        [
            proj_piece.reshape(group_xz, half // group_xz, full),
            jnp.broadcast_to(loss_part, (group_xz, 1, full)),
        ],
        axis=1,
    )
    summed = jnp.sum(exchange(blocks, XZ), axis=0)
    loss = summed[-1, 0] / (rows * group(DP))
    grad_proj = lax.all_gather(
        gather(summed[:-1], XZ).reshape(half, full), "c", axis=0, tiled=True
    )
    return (grad_hidden, grad_proj, loss)


def solution(mesh):
    fine = Mesh(mesh.devices.reshape([SIZES[axis] for axis in DP + FS]), DP + FS)
    return jax.shard_map(
        body,
        mesh=fine,
        in_specs=(P(DP, FS), P(DP, FS), P(FS, None)),
        out_specs=(P(DP, FS), P(FS, None), P()),
        check_vma=False,
    )
```

```python
import jax
import jax.numpy as jnp
from jax import lax
from jax.sharding import Mesh
from jax.sharding import PartitionSpec as P

EPSILON = 1e-06
DP = ("x", "zl", "c")
FS = ("zh", "y")
XZ = ("x", "zl")
SIZES = {"x": 4, "zl": 4, "c": 2, "zh": 2, "y": 8}
SWAP = [(0, 1), (1, 0)]
ROWS_T = (((1,), (1,)), ((), ()))
COLS_T = (((0,), (0,)), ((), ()))


def dot(a, b, dims=(((1,), (0,)), ((), ()))):
    return lax.dot_general(a, b, dims, preferred_element_type=jnp.float32)


def group(axes):
    total = 1
    for axis in axes:
        total *= SIZES[axis]
    return total


def exchange(blocks, axes):
    return lax.all_to_all(blocks, axes, split_axis=0, concat_axis=0, tiled=True)


def gather(block, axes):
    copies = jnp.broadcast_to(block[None], (group(axes),) + block.shape)
    return exchange(copies, axes)


def pieces(value):
    high = lax.reduce_precision(value, 8, 7)
    rest = value - high
    middle = lax.reduce_precision(rest, 8, 7)
    low = rest - middle
    return [part.astype(jnp.bfloat16) for part in (high, middle, low)]


def normal(values, axes):
    total = jnp.sum(values * values, axis=axes, keepdims=True)
    return (values * lax.rsqrt(total + EPSILON)).astype(jnp.bfloat16)


def around(block, axis):
    blocks = [block]
    for step in (1, 2, 3):
        blocks.append(lax.ppermute(block, axis, [(at, at ^ step) for at in range(4)]))
    return jnp.concatenate(blocks, axis=0)


def in_order(values):
    shape = values.shape
    values = values.reshape(2, 2, 2, 2, -1, shape[1])
    for dim, (axis, bit) in enumerate((("x", 2), ("x", 1), ("zl", 2), ("zl", 1))):
        swap = (lax.axis_index(axis) & bit) != 0
        values = jnp.where(swap, jnp.flip(values, dim), values)
    return values.reshape(shape)


def body(hidden, teacher, projector):
    rows, width = hidden.shape
    full = projector.shape[1]
    group_fs, group_xz = group(FS), group(XZ)
    mine = rows // group_fs
    half = width // 2
    width_t = teacher.shape[1]
    core = lax.axis_index("c")

    partial_embed = dot(hidden, projector).astype(jnp.bfloat16)
    sent = jnp.concatenate(
        [
            partial_embed.reshape(group_fs, mine, full),
            teacher.reshape(group_fs, mine, width_t),
        ],
        axis=2,
    )
    got = exchange(sent, FS)
    embed = jnp.sum(got[:, :, :full].astype(jnp.float32), axis=0)
    inv_student = lax.rsqrt(jnp.sum(embed * embed, axis=1, keepdims=True) + EPSILON)
    unit = embed * inv_student
    student = unit.astype(jnp.bfloat16)
    target = normal(got[:, :, full:].astype(jnp.float32), (0, 2))
    target = target.transpose(1, 0, 2).reshape(mine, -1)

    here = gather(jnp.concatenate([student, -target], axis=1), FS).reshape(rows, -1)
    row_block = around(around(jnp.concatenate([student, target], axis=1), "zl"), "x")
    hidden_there = lax.ppermute(hidden, "c", SWAP)
    columns = jnp.concatenate([here, lax.ppermute(here, "c", SWAP)], axis=0)
    s_cols = columns[:, :full]
    differ = dot(row_block, columns, ROWS_T)
    differ = in_order(differ)
    squares = jnp.sum(differ * differ)
    squares = squares + lax.ppermute(squares, "c", SWAP)
    partial_grad = sum(dot(part, s_cols) for part in pieces(differ)[::-1])
    partial_grad = partial_grad.astype(jnp.bfloat16).reshape(group_xz, mine, full)
    grad_unit = 4.0 * jnp.sum(exchange(partial_grad, XZ).astype(jnp.float32), axis=0)
    radial = jnp.sum(unit * grad_unit, axis=1, keepdims=True)
    grad_embed = (inv_student * (grad_unit - unit * radial)).astype(jnp.bfloat16)

    lane = lax.broadcasted_iota(jnp.int32, (mine, 128), 1)
    tail = jnp.zeros((mine, 128), jnp.bfloat16)
    for index, part in enumerate(pieces(squares)):
        tail = jnp.where(lane == index, part, tail)
    wide = gather(jnp.concatenate([grad_embed, tail], axis=1), FS).reshape(rows, -1)
    piece = wide[:, :full]
    piece_there = lax.ppermute(piece, "c", SWAP)
    grad_hidden = dot(piece, projector, ROWS_T)

    left = lax.dynamic_slice_in_dim(hidden, core * half, half, 1)
    left_there = lax.dynamic_slice_in_dim(hidden_there, core * half, half, 1)
    proj_piece = dot(left, piece, COLS_T) + dot(left_there, piece_there, COLS_T)

    loss_part = jnp.sum(
        wide.reshape(group_fs, mine, -1)[:, 0, full:].astype(jnp.float32)
    )
    blocks = jnp.concatenate(
        [
            proj_piece.reshape(group_xz, half // group_xz, full),
            jnp.broadcast_to(loss_part, (group_xz, 1, full)),
        ],
        axis=1,
    )
    summed = jnp.sum(exchange(blocks, XZ), axis=0)
    loss = summed[-1, 0] / (rows * group(DP))
    grad_proj = lax.all_gather(
        gather(summed[:-1], XZ).reshape(half, full), "c", axis=0, tiled=True
    )
    return (grad_hidden, grad_proj, loss)


def solution(mesh):
    fine = Mesh(mesh.devices.reshape([SIZES[axis] for axis in DP + FS]), DP + FS)
    return jax.shard_map(
        body,
        mesh=fine,
        in_specs=(P(DP, FS), P(DP, FS), P(FS, None)),
        out_specs=(P(DP, FS), P(FS, None), P()),
        check_vma=False,
    )
```

```python
import jax
import jax.numpy as jnp
from jax import lax
from jax.sharding import Mesh
from jax.sharding import PartitionSpec as P

EPSILON = 1e-06
DP = ("x", "zl", "c")
FS = ("zh", "y")
XZ = ("x", "zl")
SIZES = {"x": 4, "zl": 4, "c": 2, "zh": 2, "y": 8}
SWAP = [(0, 1), (1, 0)]
ROWS_T = (((1,), (1,)), ((), ()))
COLS_T = (((0,), (0,)), ((), ()))


def dot(a, b, dims=(((1,), (0,)), ((), ()))):
    return lax.dot_general(a, b, dims, preferred_element_type=jnp.float32)


def group(axes):
    total = 1
    for axis in axes:
        total *= SIZES[axis]
    return total


def exchange(blocks, axes):
    return lax.all_to_all(blocks, axes, split_axis=0, concat_axis=0, tiled=True)


def gather(block, axes):
    copies = jnp.broadcast_to(block[None], (group(axes),) + block.shape)
    return exchange(copies, axes)


def pieces(value):
    high = lax.reduce_precision(value, 8, 7)
    rest = value - high
    middle = lax.reduce_precision(rest, 8, 7)
    low = rest - middle
    return [part.astype(jnp.bfloat16) for part in (high, middle, low)]


def normal(values, axes):
    total = jnp.sum(values * values, axis=axes, keepdims=True)
    return (values * lax.rsqrt(total + EPSILON)).astype(jnp.bfloat16)


def spread(value, shape):
    lane = lax.broadcasted_iota(jnp.int32, shape, 1)
    lanes = jnp.zeros(shape, jnp.bfloat16)
    for index, part in enumerate(pieces(value)):
        lanes = jnp.where(lane == index, part, lanes)
    return lanes


def around(block, axis):
    blocks = [block]
    for step in (1, 2, 3):
        blocks.append(lax.ppermute(block, axis, [(at, at ^ step) for at in range(4)]))
    return jnp.concatenate(blocks, axis=0)


def in_order(values):
    shape = values.shape
    values = values.reshape(2, 2, 2, 2, -1, shape[1])
    for dim, (axis, bit) in enumerate((("x", 2), ("x", 1), ("zl", 2), ("zl", 1))):
        swap = (lax.axis_index(axis) & bit) != 0
        values = jnp.where(swap, jnp.flip(values, dim), values)
    return values.reshape(shape)


def body(hidden, teacher, projector):
    rows, width = hidden.shape
    full = projector.shape[1]
    group_fs, group_xz = group(FS), group(XZ)
    mine = rows // group_fs
    half = width // 2
    width_t = teacher.shape[1]
    core = lax.axis_index("c")

    partial_embed = dot(hidden, projector).astype(jnp.bfloat16)
    sent = jnp.concatenate(
        [
            partial_embed.reshape(group_fs, mine, full),
            teacher.reshape(group_fs, mine, width_t),
        ],
        axis=2,
    )
    got = exchange(sent, FS)
    embed = jnp.sum(got[:, :, :full].astype(jnp.float32), axis=0)
    inv_student = lax.rsqrt(jnp.sum(embed * embed, axis=1, keepdims=True) + EPSILON)
    unit = embed * inv_student
    student = unit.astype(jnp.bfloat16)
    target = normal(got[:, :, full:].astype(jnp.float32), (0, 2))
    target = target.transpose(1, 0, 2).reshape(mine, -1)

    both, hidden_sent = lax.optimization_barrier(
        (jnp.concatenate([student, target], axis=1), hidden)
    )
    here = gather(jnp.concatenate([student, -target], axis=1), FS).reshape(rows, -1)
    hidden_there = lax.ppermute(hidden_sent, "c", SWAP)
    both, hidden_there = lax.optimization_barrier((both, hidden_there))
    row_block = around(around(both, "zl"), "x")
    columns = jnp.concatenate([here, lax.ppermute(here, "c", SWAP)], axis=0)
    s_cols = columns[:, :full]
    differ = dot(row_block, columns, ROWS_T)
    differ = in_order(differ)
    squares = jnp.sum(differ * differ)
    squares = squares + lax.ppermute(squares, "c", SWAP)
    partial_grad = sum(dot(part, s_cols) for part in pieces(differ)[::-1])
    partial_grad = partial_grad.astype(jnp.bfloat16).reshape(group_xz, mine, full)
    grad_unit = 4.0 * jnp.sum(exchange(partial_grad, XZ).astype(jnp.float32), axis=0)
    radial = jnp.sum(unit * grad_unit, axis=1, keepdims=True)
    grad_embed = (inv_student * (grad_unit - unit * radial)).astype(jnp.bfloat16)

    wide = gather(
        jnp.concatenate([grad_embed, spread(squares, (mine, 128))], axis=1), FS
    ).reshape(rows, -1)
    piece = wide[:, :full]
    piece_there = lax.ppermute(piece, "c", SWAP)
    grad_hidden = dot(piece, projector, ROWS_T)

    left = lax.dynamic_slice_in_dim(hidden, core * half, half, 1)
    left_there = lax.dynamic_slice_in_dim(hidden_there, core * half, half, 1)
    proj_piece = dot(left, piece, COLS_T) + dot(left_there, piece_there, COLS_T)

    loss_part = jnp.sum(
        wide.reshape(group_fs, mine, -1)[:, 0, full:].astype(jnp.float32)
    )
    blocks = jnp.concatenate(
        [
            proj_piece.astype(jnp.bfloat16).reshape(group_xz, half // group_xz, full),
            jnp.broadcast_to(spread(loss_part, (1, full)), (group_xz, 1, full)),
        ],
        axis=1,
    )
    summed = jnp.sum(exchange(blocks, XZ).astype(jnp.float32), axis=0)
    loss = jnp.sum(summed[-1]) / (rows * group(DP))
    summed = summed[:-1].astype(jnp.bfloat16)
    grad_proj = lax.all_gather(
        gather(summed, XZ).reshape(half, full), "c", axis=0, tiled=True
    ).astype(jnp.float32)
    return (grad_hidden, grad_proj, loss)


def solution(mesh):
    fine = Mesh(mesh.devices.reshape([SIZES[axis] for axis in DP + FS]), DP + FS)
    return jax.shard_map(
        body,
        mesh=fine,
        in_specs=(P(DP, FS), P(DP, FS), P(FS, None)),
        out_specs=(P(DP, FS), P(FS, None), P()),
        check_vma=False,
    )
```

```python
import jax
import jax.numpy as jnp
from jax import lax
from jax.sharding import Mesh
from jax.sharding import PartitionSpec as P

EPSILON = 1e-06
DP = ("x", "zl", "c")
FS = ("zh", "y")
XZ = ("x", "zl")
SIZES = {"x": 4, "zl": 4, "c": 2, "zh": 2, "y": 8}
SWAP = [(0, 1), (1, 0)]
ROWS_T = (((1,), (1,)), ((), ()))
COLS_T = (((0,), (0,)), ((), ()))


def dot(a, b, dims=(((1,), (0,)), ((), ()))):
    return lax.dot_general(a, b, dims, preferred_element_type=jnp.float32)


def group(axes):
    total = 1
    for axis in axes:
        total *= SIZES[axis]
    return total


def exchange(blocks, axes):
    return lax.all_to_all(blocks, axes, split_axis=0, concat_axis=0, tiled=True)


def gather(block, axes):
    copies = jnp.broadcast_to(block[None], (group(axes),) + block.shape)
    return exchange(copies, axes)


def pieces(value):
    high = lax.reduce_precision(value, 8, 7)
    rest = value - high
    middle = lax.reduce_precision(rest, 8, 7)
    low = rest - middle
    return [part.astype(jnp.bfloat16) for part in (high, middle, low)]


def normal(values, axes):
    total = jnp.sum(values * values, axis=axes, keepdims=True)
    return (values * lax.rsqrt(total + EPSILON)).astype(jnp.bfloat16)


def wide_rows(blocks):
    return blocks.transpose(1, 0, 2).reshape(blocks.shape[1], -1)


def spread(value, shape):
    lane = lax.broadcasted_iota(jnp.int32, shape, 1)
    lanes = jnp.zeros(shape, jnp.bfloat16)
    for index, part in enumerate(pieces(value)):
        lanes = jnp.where(lane == index, part, lanes)
    return lanes


def around(block, axis):
    blocks = [block]
    for step in (1, 2, 3):
        blocks.append(lax.ppermute(block, axis, [(at, at ^ step) for at in range(4)]))
    return jnp.concatenate(blocks, axis=0)


def in_order(values):
    shape = values.shape
    values = values.reshape(2, 2, 2, 2, -1, shape[1])
    for dim, (axis, bit) in enumerate((("x", 2), ("x", 1), ("zl", 2), ("zl", 1))):
        swap = (lax.axis_index(axis) & bit) != 0
        values = jnp.where(swap, jnp.flip(values, dim), values)
    return values.reshape(shape)


def body(hidden, teacher, projector):
    rows, width = hidden.shape
    full = projector.shape[1]
    group_fs, group_xz = group(FS), group(XZ)
    mine = rows // group_fs
    half = width // 2
    width_t = teacher.shape[1]
    core = lax.axis_index("c")

    lanes = width_t
    deep = full // lanes
    partial_embed = dot(hidden, projector).astype(jnp.bfloat16)
    partial_embed = partial_embed.reshape(group_fs, mine, deep, lanes)
    partial_embed = partial_embed.transpose(0, 2, 1, 3).reshape(group_fs, -1, lanes)
    copies = jnp.broadcast_to(teacher[None], (group_fs,) + teacher.shape)
    got = exchange(jnp.concatenate([partial_embed, copies], axis=1), FS)
    cut = deep * mine

    embed = jnp.sum(got[:, :cut].astype(jnp.float32), axis=0)
    embed = embed.reshape(deep, mine, lanes).transpose(1, 0, 2).reshape(mine, full)
    inv_student = lax.rsqrt(jnp.sum(embed * embed, axis=1, keepdims=True) + EPSILON)
    unit = embed * inv_student
    student = unit.astype(jnp.bfloat16)
    teach_mine = lax.dynamic_slice_in_dim(got, cut + lax.axis_index(FS) * mine, mine, 1)
    target_mine = wide_rows(normal(teach_mine.astype(jnp.float32), (0, 2)))

    near = around(jnp.concatenate([student, target_mine], axis=1), "zl")
    near, got = lax.optimization_barrier((near, got))
    row_block = around(near, "x")
    s_here = gather(student, FS).reshape(rows, full)
    target = wide_rows(normal(got[:, cut:].astype(jnp.float32), (0, 2)))
    hidden_there = lax.ppermute(hidden, "c", SWAP)
    target, hidden_there = lax.optimization_barrier((target, hidden_there))
    s_cols = jnp.concatenate([s_here, lax.ppermute(s_here, "c", SWAP)], axis=0)
    t_cols = jnp.concatenate([target, lax.ppermute(target, "c", SWAP)], axis=0)
    s_rows, t_rows = row_block[:, :full], row_block[:, full:]
    differ = dot(s_rows, s_cols, ROWS_T) - dot(t_rows, t_cols, ROWS_T)
    differ = in_order(differ)
    squares = jnp.sum(differ * differ)
    squares = squares + lax.ppermute(squares, "c", SWAP)
    partial_grad = sum(dot(part, s_cols) for part in pieces(differ)[::-1])
    partial_grad = partial_grad.astype(jnp.bfloat16).reshape(group_xz, mine, full)
    grad_unit = 4.0 * jnp.sum(exchange(partial_grad, XZ).astype(jnp.float32), axis=0)
    radial = jnp.sum(unit * grad_unit, axis=1, keepdims=True)
    grad_embed = (inv_student * (grad_unit - unit * radial)).astype(jnp.bfloat16)

    wide = gather(
        jnp.concatenate([grad_embed, spread(squares, (mine, 128))], axis=1), FS
    ).reshape(rows, -1)
    piece = wide[:, :full]
    piece_there = lax.ppermute(piece, "c", SWAP)
    grad_hidden = dot(piece, projector, ROWS_T)

    left = lax.dynamic_slice_in_dim(hidden, core * half, half, 1)
    left_there = lax.dynamic_slice_in_dim(hidden_there, core * half, half, 1)
    proj_piece = dot(left, piece, COLS_T) + dot(left_there, piece_there, COLS_T)

    loss_part = jnp.sum(
        wide.reshape(group_fs, mine, -1)[:, 0, full:].astype(jnp.float32)
    )
    blocks = jnp.concatenate(
        [
            proj_piece.astype(jnp.bfloat16).reshape(group_xz, half // group_xz, full),
            jnp.broadcast_to(spread(loss_part, (1, full)), (group_xz, 1, full)),
        ],
        axis=1,
    )
    summed = jnp.sum(exchange(blocks, XZ).astype(jnp.float32), axis=0)
    loss = jnp.sum(summed[-1]) / (rows * group(DP))
    summed = summed[:-1].astype(jnp.bfloat16)
    grad_proj = lax.all_gather(
        gather(summed, XZ).reshape(half, full), "c", axis=0, tiled=True
    ).astype(jnp.float32)
    return (grad_hidden, grad_proj, loss)


def solution(mesh):
    fine = Mesh(mesh.devices.reshape([SIZES[axis] for axis in DP + FS]), DP + FS)
    return jax.shard_map(
        body,
        mesh=fine,
        in_specs=(P(DP, FS), P(DP, FS), P(FS, None)),
        out_specs=(P(DP, FS), P(FS, None), P()),
        check_vma=False,
    )
```

```python
import jax
import jax.numpy as jnp
from jax import lax
from jax.sharding import Mesh
from jax.sharding import PartitionSpec as P

EPSILON = 1e-06
DP = ("x", "zl", "c")
FS = ("zh", "y")
XZ = ("x", "zl")
SIZES = {"x": 4, "zl": 4, "c": 2, "zh": 2, "y": 8}
SWAP = [(0, 1), (1, 0)]
ROWS_T = (((1,), (1,)), ((), ()))
COLS_T = (((0,), (0,)), ((), ()))


def dot(a, b, dims=(((1,), (0,)), ((), ()))):
    return lax.dot_general(a, b, dims, preferred_element_type=jnp.float32)


def group(axes):
    total = 1
    for axis in axes:
        total *= SIZES[axis]
    return total


def exchange(blocks, axes):
    return lax.all_to_all(blocks, axes, split_axis=0, concat_axis=0, tiled=True)


def gather(block, axes):
    copies = jnp.broadcast_to(block[None], (group(axes),) + block.shape)
    return exchange(copies, axes)


def pieces(value):
    high = lax.reduce_precision(value, 8, 7)
    rest = value - high
    middle = lax.reduce_precision(rest, 8, 7)
    low = rest - middle
    return [part.astype(jnp.bfloat16) for part in (high, middle, low)]


def normal(values, axes):
    total = jnp.sum(values * values, axis=axes, keepdims=True)
    return (values * lax.rsqrt(total + EPSILON)).astype(jnp.bfloat16)


def spread(value, shape):
    lane = lax.broadcasted_iota(jnp.int32, shape, 1)
    lanes = jnp.zeros(shape, jnp.bfloat16)
    for index, part in enumerate(pieces(value)):
        lanes = jnp.where(lane == index, part, lanes)
    return lanes


def around(block, axis):
    blocks = [block]
    for step in (1, 2, 3):
        blocks.append(lax.ppermute(block, axis, [(at, at ^ step) for at in range(4)]))
    return jnp.concatenate(blocks, axis=0)


def in_order(values):
    shape = values.shape
    values = values.reshape(2, 2, 2, 2, -1, shape[1])
    for dim, (axis, bit) in enumerate((("x", 2), ("x", 1), ("zl", 2), ("zl", 1))):
        swap = (lax.axis_index(axis) & bit) != 0
        values = jnp.where(swap, jnp.flip(values, dim), values)
    return values.reshape(shape)


def body(hidden, teacher, projector):
    rows, width = hidden.shape
    full = projector.shape[1]
    group_fs, group_xz = group(FS), group(XZ)
    mine = rows // group_fs
    half = width // 2
    width_t = teacher.shape[1]
    core = lax.axis_index("c")

    partial_embed = dot(hidden, projector).astype(jnp.bfloat16)
    sent = jnp.concatenate(
        [
            partial_embed.reshape(group_fs, mine, full),
            teacher.reshape(group_fs, mine, width_t),
        ],
        axis=2,
    )
    got = exchange(sent, FS)
    embed = jnp.sum(got[:, :, :full].astype(jnp.float32), axis=0)
    inv_student = lax.rsqrt(jnp.sum(embed * embed, axis=1, keepdims=True) + EPSILON)
    unit = embed * inv_student
    student = unit.astype(jnp.bfloat16)
    target = normal(got[:, :, full:].astype(jnp.float32), (0, 2))
    target = target.transpose(1, 0, 2).reshape(mine, -1)

    near = around(jnp.concatenate([student, target], axis=1), "zl")
    mine_cols = jnp.concatenate([student, -target], axis=1)
    pair = jnp.concatenate([mine_cols, lax.ppermute(mine_cols, "zh", SWAP)], axis=0)
    here = gather(pair, ("y",)).reshape(rows, -1)
    _, hidden_sent = lax.optimization_barrier((pair, hidden))
    hidden_there = lax.ppermute(hidden_sent, "c", SWAP)
    near, hidden_there = lax.optimization_barrier((near, hidden_there))
    row_block = around(near, "x")
    here, row_block = lax.optimization_barrier((here, row_block))
    columns = jnp.concatenate([here, lax.ppermute(here, "c", SWAP)], axis=0)
    s_cols = columns[:, :full]
    differ = dot(row_block, columns, ROWS_T)
    differ = in_order(differ)
    squares = jnp.sum(differ * differ)
    squares = squares + lax.ppermute(squares, "c", SWAP)
    partial_grad = sum(dot(part, s_cols) for part in pieces(differ)[::-1])
    partial_grad = partial_grad.astype(jnp.bfloat16).reshape(group_xz, mine, full)
    grad_unit = 4.0 * jnp.sum(exchange(partial_grad, XZ).astype(jnp.float32), axis=0)
    radial = jnp.sum(unit * grad_unit, axis=1, keepdims=True)
    grad_embed = (inv_student * (grad_unit - unit * radial)).astype(jnp.bfloat16)

    wide = gather(
        jnp.concatenate([grad_embed, spread(squares, (mine, 128))], axis=1), FS
    ).reshape(rows, -1)
    piece = wide[:, :full]
    piece_there = lax.ppermute(piece, "c", SWAP)
    grad_hidden = dot(piece, projector, ROWS_T)

    left = lax.dynamic_slice_in_dim(hidden, core * half, half, 1)
    left_there = lax.dynamic_slice_in_dim(hidden_there, core * half, half, 1)
    proj_piece = dot(left, piece, COLS_T) + dot(left_there, piece_there, COLS_T)

    loss_part = jnp.sum(
        wide.reshape(group_fs, mine, -1)[:, 0, full:].astype(jnp.float32)
    )
    blocks = jnp.concatenate(
        [
            proj_piece.astype(jnp.bfloat16).reshape(group_xz, half // group_xz, full),
            jnp.broadcast_to(spread(loss_part, (1, full)), (group_xz, 1, full)),
        ],
        axis=1,
    )
    summed = jnp.sum(exchange(blocks, XZ).astype(jnp.float32), axis=0)
    loss = jnp.sum(summed[-1]) / (rows * group(DP))
    summed = summed[:-1].astype(jnp.bfloat16)
    grad_proj = lax.all_gather(
        gather(summed, XZ).reshape(half, full), "c", axis=0, tiled=True
    ).astype(jnp.float32)
    return (grad_hidden, grad_proj, loss)


def solution(mesh):
    fine = Mesh(mesh.devices.reshape([SIZES[axis] for axis in DP + FS]), DP + FS)
    return jax.shard_map(
        body,
        mesh=fine,
        in_specs=(P(DP, FS), P(DP, FS), P(FS, None)),
        out_specs=(P(DP, FS), P(FS, None), P()),
        check_vma=False,
    )
```

```python
import jax
import jax.numpy as jnp
from jax import lax
from jax.sharding import Mesh
from jax.sharding import PartitionSpec as P

EPSILON = 1e-06
DP = ("x", "zl", "c")
FS = ("zh", "y")
XZ = ("x", "zl")
SIZES = {"x": 4, "zl": 4, "c": 2, "zh": 2, "y": 8}
SWAP = [(0, 1), (1, 0)]
ROWS_T = (((1,), (1,)), ((), ()))
COLS_T = (((0,), (0,)), ((), ()))


def dot(a, b, dims=(((1,), (0,)), ((), ()))):
    return lax.dot_general(a, b, dims, preferred_element_type=jnp.float32)


def group(axes):
    total = 1
    for axis in axes:
        total *= SIZES[axis]
    return total


def exchange(blocks, axes):
    return lax.all_to_all(blocks, axes, split_axis=0, concat_axis=0, tiled=True)


def gather(block, axes):
    copies = jnp.broadcast_to(block[None], (group(axes),) + block.shape)
    return exchange(copies, axes)


def pieces(value):
    high = lax.reduce_precision(value, 8, 7)
    rest = value - high
    middle = lax.reduce_precision(rest, 8, 7)
    low = rest - middle
    return [part.astype(jnp.bfloat16) for part in (high, middle, low)]


def normal(values, axes):
    total = jnp.sum(values * values, axis=axes, keepdims=True)
    return (values * lax.rsqrt(total + EPSILON)).astype(jnp.bfloat16)


def spread(value, shape, place):
    lane = lax.broadcasted_iota(jnp.int32, shape, 1) - 3 * place
    lanes = jnp.zeros(shape, jnp.bfloat16)
    for index, part in enumerate(pieces(value)):
        lanes = jnp.where(lane == index, part, lanes)
    return lanes


def around(block, axis):
    blocks = [block]
    for step in (1, 2, 3):
        blocks.append(lax.ppermute(block, axis, [(at, at ^ step) for at in range(4)]))
    return jnp.concatenate(blocks, axis=0)


def in_order(values):
    shape = values.shape
    values = values.reshape(2, 2, 2, 2, -1, shape[1])
    for dim, (axis, bit) in enumerate((("x", 2), ("x", 1), ("zl", 2), ("zl", 1))):
        swap = (lax.axis_index(axis) & bit) != 0
        values = jnp.where(swap, jnp.flip(values, dim), values)
    return values.reshape(shape)


def body(hidden, teacher, projector):
    rows, width = hidden.shape
    full = projector.shape[1]
    group_fs, group_xz = group(FS), group(XZ)
    mine = rows // group_fs
    half = width // 2
    width_t = teacher.shape[1]
    core = lax.axis_index("c")

    partial_embed = dot(hidden, projector).astype(jnp.bfloat16)
    sent = jnp.concatenate(
        [
            partial_embed.reshape(group_fs, mine, full),
            teacher.reshape(group_fs, mine, width_t),
        ],
        axis=2,
    )
    got = exchange(sent, FS)
    embed = jnp.sum(got[:, :, :full].astype(jnp.float32), axis=0)
    inv_student = lax.rsqrt(jnp.sum(embed * embed, axis=1, keepdims=True) + EPSILON)
    unit = embed * inv_student
    student = unit.astype(jnp.bfloat16)
    target = normal(got[:, :, full:].astype(jnp.float32), (0, 2))
    target = target.transpose(1, 0, 2).reshape(mine, -1)

    near = around(jnp.concatenate([student, target], axis=1), "zl")
    mine_cols = jnp.concatenate([student, -target], axis=1)
    pair = jnp.concatenate([mine_cols, lax.ppermute(mine_cols, "zh", SWAP)], axis=0)
    pair, near, hidden_sent = lax.optimization_barrier((pair, near, hidden))
    here = gather(pair, ("y",)).reshape(rows, -1)
    hidden_there = lax.ppermute(hidden_sent, "c", SWAP)
    near, hidden_there = lax.optimization_barrier((near, hidden_there))
    row_block = around(near, "x")
    here, row_block = lax.optimization_barrier((here, row_block))
    columns = jnp.concatenate([here, lax.ppermute(here, "c", SWAP)], axis=0)
    s_cols = columns[:, :full]
    differ = dot(row_block, columns, ROWS_T)
    differ = in_order(differ)
    squares = jnp.sum(differ * differ)
    squares = squares + lax.ppermute(squares, "c", SWAP)
    partial_grad = sum(dot(part, s_cols) for part in pieces(differ)[::-1])
    partial_grad = partial_grad.astype(jnp.bfloat16).reshape(group_xz, mine, full)
    grad_unit = 4.0 * jnp.sum(exchange(partial_grad, XZ).astype(jnp.float32), axis=0)
    radial = jnp.sum(unit * grad_unit, axis=1, keepdims=True)
    grad_embed = (inv_student * (grad_unit - unit * radial)).astype(jnp.bfloat16)

    wide = gather(
        jnp.concatenate([grad_embed, spread(squares, (mine, 128), lax.axis_index(FS))], axis=1), FS
    ).reshape(rows, -1)
    piece = wide[:, :full]
    piece_there = lax.ppermute(piece, "c", SWAP)
    grad_hidden = dot(piece, projector, ROWS_T)

    left = lax.dynamic_slice_in_dim(hidden, core * half, half, 1)
    left_there = lax.dynamic_slice_in_dim(hidden_there, core * half, half, 1)
    proj_piece = dot(left, piece, COLS_T) + dot(left_there, piece_there, COLS_T)

    loss_row = jnp.sum(
        wide.reshape(group_fs, mine, -1)[:, 0, full:].astype(jnp.float32), axis=0
    )
    loss_row = jnp.pad(loss_row.astype(jnp.bfloat16), (0, full - 128))
    blocks = jnp.concatenate(
        [
            proj_piece.astype(jnp.bfloat16).reshape(group_xz, half // group_xz, full),
            jnp.broadcast_to(loss_row, (group_xz, 1, full)),
        ],
        axis=1,
    )
    summed = jnp.sum(exchange(blocks, XZ).astype(jnp.float32), axis=0)
    loss = jnp.sum(summed[-1]) / (rows * group(DP))
    summed = summed[:-1].astype(jnp.bfloat16)
    grad_proj = lax.all_gather(
        gather(summed, XZ).reshape(half, full), "c", axis=0, tiled=True
    ).astype(jnp.float32)
    return (grad_hidden, grad_proj, loss)


def solution(mesh):
    fine = Mesh(mesh.devices.reshape([SIZES[axis] for axis in DP + FS]), DP + FS)
    return jax.shard_map(
        body,
        mesh=fine,
        in_specs=(P(DP, FS), P(DP, FS), P(FS, None)),
        out_specs=(P(DP, FS), P(FS, None), P()),
        check_vma=False,
    )
```

```python
import jax
import jax.numpy as jnp
from jax import lax
from jax.sharding import Mesh
from jax.sharding import PartitionSpec as P

EPSILON = 1e-06
DP = ("x", "zl", "c")
FS = ("zh", "y")
XZ = ("x", "zl")
SIZES = {"x": 4, "zl": 4, "c": 2, "zh": 2, "y": 8}
SWAP = [(0, 1), (1, 0)]
ROWS_T = (((1,), (1,)), ((), ()))
COLS_T = (((0,), (0,)), ((), ()))


def dot(a, b, dims=(((1,), (0,)), ((), ()))):
    return lax.dot_general(a, b, dims, preferred_element_type=jnp.float32)


def group(axes):
    total = 1
    for axis in axes:
        total *= SIZES[axis]
    return total


def exchange(blocks, axes):
    return lax.all_to_all(blocks, axes, split_axis=0, concat_axis=0, tiled=True)


def gather(block, axes):
    copies = jnp.broadcast_to(block[None], (group(axes),) + block.shape)
    return exchange(copies, axes)


def pieces(value):
    high = lax.reduce_precision(value, 8, 7)
    rest = value - high
    middle = lax.reduce_precision(rest, 8, 7)
    low = rest - middle
    return [part.astype(jnp.bfloat16) for part in (high, middle, low)]


def normal(values, axes):
    total = jnp.sum(values * values, axis=axes, keepdims=True)
    return (values * lax.rsqrt(total + EPSILON)).astype(jnp.bfloat16)


def spread(value, shape, place):
    lane = lax.broadcasted_iota(jnp.int32, shape, 1) - 3 * place
    lanes = jnp.zeros(shape, jnp.bfloat16)
    for index, part in enumerate(pieces(value)):
        lanes = jnp.where(lane == index, part, lanes)
    return lanes


def around(block, axis):
    blocks = [block]
    for step in (1, 2, 3):
        blocks.append(lax.ppermute(block, axis, [(at, at ^ step) for at in range(4)]))
    return blocks


def in_order(values):
    shape = values.shape
    values = values.reshape(2, 2, 2, 2, -1, shape[1])
    for dim, (axis, bit) in enumerate((("x", 2), ("x", 1), ("zl", 2), ("zl", 1))):
        swap = (lax.axis_index(axis) & bit) != 0
        values = jnp.where(swap, jnp.flip(values, dim), values)
    return values.reshape(shape)


def body(hidden, teacher, projector):
    rows, width = hidden.shape
    full = projector.shape[1]
    group_fs, group_xz = group(FS), group(XZ)
    mine = rows // group_fs
    half = width // 2
    width_t = teacher.shape[1]
    core = lax.axis_index("c")

    over = lax.ppermute(teacher, "zh", SWAP)
    first = lax.axis_index("zh") == 0
    both = jnp.concatenate(
        [jnp.where(first, teacher, over), jnp.where(first, over, teacher)], axis=1
    )
    teach = lax.all_gather(both, "y", axis=0)

    partial_embed = dot(hidden, projector).astype(jnp.bfloat16)
    sent = jnp.concatenate(
        [
            partial_embed.reshape(group_fs, mine, full),
            teacher.reshape(group_fs, mine, width_t),
        ],
        axis=2,
    )
    got = exchange(sent, FS)
    embed = jnp.sum(got[:, :, :full].astype(jnp.float32), axis=0)
    inv_student = lax.rsqrt(jnp.sum(embed * embed, axis=1, keepdims=True) + EPSILON)
    unit = embed * inv_student
    student = unit.astype(jnp.bfloat16)
    target_mine = (
        normal(got[:, :, full:].astype(jnp.float32), (0, 2))
        .reshape(SIZES["zh"], SIZES["y"], mine, width_t)
        .transpose(2, 1, 0, 3)
        .reshape(mine, -1)
    )

    near = jnp.concatenate(
        around(jnp.concatenate([student, target_mine], axis=1), "zl"), axis=0
    )
    student_sent, near, hidden_sent = lax.optimization_barrier((student, near, hidden))
    s_here = gather(student_sent, FS).reshape(rows, full)
    hidden_there = lax.ppermute(hidden_sent, "c", SWAP)
    near, hidden_there = lax.optimization_barrier((near, hidden_there))
    far = around(near, "x")
    far[1], teach = lax.optimization_barrier((far[1], teach))
    target = normal(teach.astype(jnp.float32), (0, 2)).transpose(1, 0, 2)
    target = target.reshape(rows, -1)
    t_cols = jnp.concatenate([target, lax.ppermute(target, "c", SWAP)], axis=0)
    row_block = jnp.concatenate(far, axis=0)
    s_here, row_block = lax.optimization_barrier((s_here, row_block))
    s_cols = jnp.concatenate([s_here, lax.ppermute(s_here, "c", SWAP)], axis=0)
    s_rows, t_rows = row_block[:, :full], row_block[:, full:]
    differ = dot(s_rows, s_cols, ROWS_T) - dot(t_rows, t_cols, ROWS_T)
    differ = in_order(differ)
    squares = jnp.sum(differ * differ)
    squares = squares + lax.ppermute(squares, "c", SWAP)
    partial_grad = sum(dot(part, s_cols) for part in pieces(differ)[::-1])
    partial_grad = partial_grad.astype(jnp.bfloat16).reshape(group_xz, mine, full)
    grad_unit = 4.0 * jnp.sum(exchange(partial_grad, XZ).astype(jnp.float32), axis=0)
    radial = jnp.sum(unit * grad_unit, axis=1, keepdims=True)
    grad_embed = (inv_student * (grad_unit - unit * radial)).astype(jnp.bfloat16)

    wide = gather(
        jnp.concatenate([grad_embed, spread(squares, (mine, 128), lax.axis_index(FS))], axis=1), FS
    ).reshape(rows, -1)
    piece = wide[:, :full]
    piece_there = lax.ppermute(piece, "c", SWAP)
    grad_hidden = dot(piece, projector, ROWS_T)

    left = lax.dynamic_slice_in_dim(hidden, core * half, half, 1)
    left_there = lax.dynamic_slice_in_dim(hidden_there, core * half, half, 1)
    proj_piece = dot(left, piece, COLS_T) + dot(left_there, piece_there, COLS_T)

    loss_row = jnp.sum(
        wide.reshape(group_fs, mine, -1)[:, 0, full:].astype(jnp.float32), axis=0
    )
    loss_row = jnp.pad(loss_row.astype(jnp.bfloat16), (0, full - 128))
    blocks = jnp.concatenate(
        [
            proj_piece.astype(jnp.bfloat16).reshape(group_xz, half // group_xz, full),
            jnp.broadcast_to(loss_row, (group_xz, 1, full)),
        ],
        axis=1,
    )
    summed = jnp.sum(exchange(blocks, XZ).astype(jnp.float32), axis=0)
    loss = jnp.sum(summed[-1]) / (rows * group(DP))
    summed = summed[:-1].astype(jnp.bfloat16)
    grad_proj = lax.all_gather(
        gather(summed, XZ).reshape(half, full), "c", axis=0, tiled=True
    ).astype(jnp.float32)
    return (grad_hidden, grad_proj, loss)


def solution(mesh):
    fine = Mesh(mesh.devices.reshape([SIZES[axis] for axis in DP + FS]), DP + FS)
    return jax.shard_map(
        body,
        mesh=fine,
        in_specs=(P(DP, FS), P(DP, FS), P(FS, None)),
        out_specs=(P(DP, FS), P(FS, None), P()),
        check_vma=False,
    )
```

```python
import jax
import jax.numpy as jnp
from jax import lax
from jax.sharding import Mesh
from jax.sharding import PartitionSpec as P

EPSILON = 1e-06
DP = ("x", "zb", "za", "c")
FS = ("zh", "y")
XZ = ("x", "zb", "za")
STRIDE = ("zb", "zh")
ROW = ("x",) + STRIDE
SIZES = {"x": 4, "zb": 2, "za": 2, "c": 2, "zh": 2, "y": 8}
SWAP = [(0, 1), (1, 0)]
ROWS_T = (((1,), (1,)), ((), ()))
COLS_T = (((0,), (0,)), ((), ()))


def dot(a, b, dims=(((1,), (0,)), ((), ()))):
    return lax.dot_general(a, b, dims, preferred_element_type=jnp.float32)


def group(axes):
    total = 1
    for axis in axes:
        total *= SIZES[axis]
    return total


def exchange(blocks, axes):
    return lax.all_to_all(blocks, axes, split_axis=0, concat_axis=0, tiled=True)


def gather(block, axes):
    copies = jnp.broadcast_to(block[None], (group(axes),) + block.shape)
    return exchange(copies, axes)


def pieces(value):
    high = lax.reduce_precision(value, 8, 7)
    rest = value - high
    middle = lax.reduce_precision(rest, 8, 7)
    low = rest - middle
    return [part.astype(jnp.bfloat16) for part in (high, middle, low)]


def normal(values, axes):
    total = jnp.sum(values * values, axis=axes, keepdims=True)
    return (values * lax.rsqrt(total + EPSILON)).astype(jnp.bfloat16)


def spread(value, shape, place):
    lane = lax.broadcasted_iota(jnp.int32, shape, 1) - 3 * place
    lanes = jnp.zeros(shape, jnp.bfloat16)
    for index, part in enumerate(pieces(value)):
        lanes = jnp.where(lane == index, part, lanes)
    return lanes


def around(block, axis):
    blocks = [block]
    for step in (1, 2, 3):
        blocks.append(lax.ppermute(block, axis, [(at, at ^ step) for at in range(4)]))
    return jnp.concatenate(blocks, axis=0)


def in_order(values):
    shape = values.shape
    values = values.reshape(2, 2, 2, 2, -1, shape[1])
    for dim, (axis, bit) in enumerate((("x", 2), ("x", 1), ("zb", 1), ("zh", 1))):
        swap = (lax.axis_index(axis) & bit) != 0
        values = jnp.where(swap, jnp.flip(values, dim), values)
    return values.reshape(shape)


def body(hidden, teacher, projector):
    rows, width = hidden.shape
    full = projector.shape[1]
    group_fs, group_xz = group(FS), group(XZ)
    mine = rows // group_fs
    half = width // 2
    width_t = teacher.shape[1]
    core = lax.axis_index("c")

    partial_embed = dot(hidden, projector).astype(jnp.bfloat16)
    sent = jnp.concatenate(
        [
            partial_embed.reshape(group_fs, mine, full),
            teacher.reshape(group_fs, mine, width_t),
        ],
        axis=2,
    )
    got = exchange(sent, FS)
    embed = jnp.sum(got[:, :, :full].astype(jnp.float32), axis=0)
    inv_student = lax.rsqrt(jnp.sum(embed * embed, axis=1, keepdims=True) + EPSILON)
    unit = embed * inv_student
    student = unit.astype(jnp.bfloat16)
    target = normal(got[:, :, full:].astype(jnp.float32), (0, 2))
    target = target.transpose(1, 0, 2).reshape(mine, -1)

    mine_rows, hidden_sent = lax.optimization_barrier(
        (jnp.concatenate([student, target], axis=1), hidden)
    )
    here = gather(jnp.concatenate([student, -target], axis=1), ("y",))
    here = here.reshape(-1, here.shape[2])
    hidden_there = lax.ppermute(hidden_sent, "c", SWAP)
    mine_rows, hidden_there = lax.optimization_barrier((mine_rows, hidden_there))
    row_block = around(around(mine_rows, STRIDE), "x")
    there = lax.ppermute(here, "za", SWAP)
    columns = jnp.concatenate(
        [here, lax.ppermute(here, "c", SWAP), there, lax.ppermute(there, "c", SWAP)],
        axis=0,
    )
    s_cols = columns[:, :full]
    differ = dot(row_block, columns, ROWS_T)
    differ = in_order(differ)
    squares = jnp.sum(differ * differ)
    squares = squares + lax.ppermute(squares, "c", SWAP)
    partial_grad = sum(dot(part, s_cols) for part in pieces(differ)[::-1])
    partial_grad = partial_grad.astype(jnp.bfloat16).reshape(-1, mine, full)
    grad_unit = 4.0 * jnp.sum(exchange(partial_grad, ROW).astype(jnp.float32), axis=0)
    radial = jnp.sum(unit * grad_unit, axis=1, keepdims=True)
    grad_embed = (inv_student * (grad_unit - unit * radial)).astype(jnp.bfloat16)

    wide = gather(
        jnp.concatenate([grad_embed, spread(squares, (mine, 128), lax.axis_index(FS))], axis=1), FS
    ).reshape(rows, -1)
    piece = wide[:, :full]
    piece_there = lax.ppermute(piece, "c", SWAP)
    grad_hidden = dot(piece, projector, ROWS_T)

    left = lax.dynamic_slice_in_dim(hidden, core * half, half, 1)
    left_there = lax.dynamic_slice_in_dim(hidden_there, core * half, half, 1)
    proj_piece = dot(left, piece, COLS_T) + dot(left_there, piece_there, COLS_T)

    loss_row = jnp.sum(
        wide.reshape(group_fs, mine, -1)[:, 0, full:].astype(jnp.float32), axis=0
    )
    loss_row = jnp.pad(loss_row.astype(jnp.bfloat16), (0, full - 128))
    blocks = jnp.concatenate(
        [
            proj_piece.astype(jnp.bfloat16).reshape(group_xz, half // group_xz, full),
            jnp.broadcast_to(loss_row, (group_xz, 1, full)),
        ],
        axis=1,
    )
    summed = jnp.sum(exchange(blocks, XZ).astype(jnp.float32), axis=0)
    loss = jnp.sum(summed[-1]) / (rows * group(DP))
    summed = summed[:-1].astype(jnp.bfloat16)
    grad_proj = lax.all_gather(
        gather(summed, XZ).reshape(half, full), "c", axis=0, tiled=True
    ).astype(jnp.float32)
    return (grad_hidden, grad_proj, loss)


def solution(mesh):
    fine = Mesh(mesh.devices.reshape([SIZES[axis] for axis in DP + FS]), DP + FS)
    return jax.shard_map(
        body,
        mesh=fine,
        in_specs=(P(DP, FS), P(DP, FS), P(FS, None)),
        out_specs=(P(DP, FS), P(FS, None), P()),
        check_vma=False,
    )
```

```python
import jax
import jax.numpy as jnp
from jax import lax
from jax.sharding import Mesh
from jax.sharding import PartitionSpec as P

EPSILON = 1e-06
DP = ("x", "zb", "za", "c")
FS = ("zh", "y")
XZ = ("x", "zb", "za")
STRIDE = ("zb", "zh")
ROW = ("x",) + STRIDE
SIZES = {"x": 4, "zb": 2, "za": 2, "c": 2, "zh": 2, "y": 8}
SWAP = [(0, 1), (1, 0)]
ROWS_T = (((1,), (1,)), ((), ()))
COLS_T = (((0,), (0,)), ((), ()))


def dot(a, b, dims=(((1,), (0,)), ((), ()))):
    return lax.dot_general(a, b, dims, preferred_element_type=jnp.float32)


def group(axes):
    total = 1
    for axis in axes:
        total *= SIZES[axis]
    return total


def exchange(blocks, axes):
    return lax.all_to_all(blocks, axes, split_axis=0, concat_axis=0, tiled=True)


def gather(block, axes):
    copies = jnp.broadcast_to(block[None], (group(axes),) + block.shape)
    return exchange(copies, axes)


def pieces(value):
    high = lax.reduce_precision(value, 8, 7)
    rest = value - high
    middle = lax.reduce_precision(rest, 8, 7)
    low = rest - middle
    return [part.astype(jnp.bfloat16) for part in (high, middle, low)]


def normal(values, axes):
    total = jnp.sum(values * values, axis=axes, keepdims=True)
    return (values * lax.rsqrt(total + EPSILON)).astype(jnp.bfloat16)


def spread(value, shape, place):
    lane = lax.broadcasted_iota(jnp.int32, shape, 1) - 3 * place
    lanes = jnp.zeros(shape, jnp.bfloat16)
    for index, part in enumerate(pieces(value)):
        lanes = jnp.where(lane == index, part, lanes)
    return lanes


def around(block, axis):
    blocks = [block]
    for step in (1, 2, 3):
        blocks.append(lax.ppermute(block, axis, [(at, at ^ step) for at in range(4)]))
    return jnp.concatenate(blocks, axis=0)


def in_order(values):
    shape = values.shape
    values = values.reshape(SIZES["x"], 2, 2, -1, shape[1])
    for dim, axis in ((1, "zb"), (2, "zh")):
        values = jnp.where(lax.axis_index(axis) != 0, jnp.flip(values, dim), values)
    return values.reshape(shape)


def body(hidden, teacher, projector):
    rows, width = hidden.shape
    full = projector.shape[1]
    group_fs, group_xz = group(FS), group(XZ)
    mine = rows // group_fs
    half = width // 2
    width_t = teacher.shape[1]
    core = lax.axis_index("c")

    partial_embed = dot(hidden, projector).astype(jnp.bfloat16)
    sent = jnp.concatenate(
        [
            partial_embed.reshape(group_fs, mine, full),
            teacher.reshape(group_fs, mine, width_t),
        ],
        axis=2,
    )
    got = exchange(sent, FS)
    embed = jnp.sum(got[:, :, :full].astype(jnp.float32), axis=0)
    inv_student = lax.rsqrt(jnp.sum(embed * embed, axis=1, keepdims=True) + EPSILON)
    unit = embed * inv_student
    student = unit.astype(jnp.bfloat16)
    target = normal(got[:, :, full:].astype(jnp.float32), (0, 2))
    target = target.transpose(1, 0, 2).reshape(mine, -1)

    mine_rows, hidden_sent = lax.optimization_barrier(
        (jnp.concatenate([student, target], axis=1), hidden)
    )
    here = gather(jnp.concatenate([student, -target], axis=1), ("y",))
    here = here.reshape(-1, here.shape[2])
    hidden_there = lax.ppermute(hidden_sent, "c", SWAP)
    mine_rows, hidden_there = lax.optimization_barrier((mine_rows, hidden_there))
    near, here = lax.optimization_barrier((around(mine_rows, STRIDE), here))
    row_block = gather(near, ("x",)).reshape(rows, -1)
    there = lax.ppermute(here, "za", SWAP)
    columns = jnp.concatenate(
        [here, lax.ppermute(here, "c", SWAP), there, lax.ppermute(there, "c", SWAP)],
        axis=0,
    )
    s_cols = columns[:, :full]
    differ = dot(row_block, columns, ROWS_T)
    differ = in_order(differ)
    squares = jnp.sum(differ * differ)
    squares = squares + lax.ppermute(squares, "c", SWAP)
    partial_grad = sum(dot(part, s_cols) for part in pieces(differ)[::-1])
    partial_grad = partial_grad.astype(jnp.bfloat16).reshape(-1, mine, full)
    grad_unit = 4.0 * jnp.sum(exchange(partial_grad, ROW).astype(jnp.float32), axis=0)
    radial = jnp.sum(unit * grad_unit, axis=1, keepdims=True)
    grad_embed = (inv_student * (grad_unit - unit * radial)).astype(jnp.bfloat16)

    wide = gather(
        jnp.concatenate([grad_embed, spread(squares, (mine, 128), lax.axis_index(FS))], axis=1), FS
    ).reshape(rows, -1)
    piece = wide[:, :full]
    piece_there = lax.ppermute(piece, "c", SWAP)
    grad_hidden = dot(piece, projector, ROWS_T)

    left = lax.dynamic_slice_in_dim(hidden, core * half, half, 1)
    left_there = lax.dynamic_slice_in_dim(hidden_there, core * half, half, 1)
    proj_piece = dot(left, piece, COLS_T) + dot(left_there, piece_there, COLS_T)

    loss_row = jnp.sum(
        wide.reshape(group_fs, mine, -1)[:, 0, full:].astype(jnp.float32), axis=0
    )
    loss_row = jnp.pad(loss_row.astype(jnp.bfloat16), (0, full - 128))
    blocks = jnp.concatenate(
        [
            proj_piece.astype(jnp.bfloat16).reshape(group_xz, half // group_xz, full),
            jnp.broadcast_to(loss_row, (group_xz, 1, full)),
        ],
        axis=1,
    )
    summed = jnp.sum(exchange(blocks, XZ).astype(jnp.float32), axis=0)
    loss = jnp.sum(summed[-1]) / (rows * group(DP))
    summed = summed[:-1].astype(jnp.bfloat16)
    grad_proj = lax.all_gather(
        gather(summed, XZ).reshape(half, full), "c", axis=0, tiled=True
    ).astype(jnp.float32)
    return (grad_hidden, grad_proj, loss)


def solution(mesh):
    fine = Mesh(mesh.devices.reshape([SIZES[axis] for axis in DP + FS]), DP + FS)
    return jax.shard_map(
        body,
        mesh=fine,
        in_specs=(P(DP, FS), P(DP, FS), P(FS, None)),
        out_specs=(P(DP, FS), P(FS, None), P()),
        check_vma=False,
    )
```

```python
import jax
import jax.numpy as jnp
from jax import lax
from jax.sharding import Mesh
from jax.sharding import PartitionSpec as P

EPSILON = 1e-06
DP = ("x", "zb", "za", "c")
FS = ("zh", "y")
XZ = ("x", "zb", "za")
STRIDE = ("zb", "zh")
ROW = ("x",) + STRIDE
SIZES = {"x": 4, "zb": 2, "za": 2, "c": 2, "zh": 2, "y": 8}
SWAP = [(0, 1), (1, 0)]
ROWS_T = (((1,), (1,)), ((), ()))
COLS_T = (((0,), (0,)), ((), ()))


def dot(a, b, dims=(((1,), (0,)), ((), ()))):
    return lax.dot_general(a, b, dims, preferred_element_type=jnp.float32)


def group(axes):
    total = 1
    for axis in axes:
        total *= SIZES[axis]
    return total


def exchange(blocks, axes):
    return lax.all_to_all(blocks, axes, split_axis=0, concat_axis=0, tiled=True)


def gather(block, axes):
    copies = jnp.broadcast_to(block[None], (group(axes),) + block.shape)
    return exchange(copies, axes)


def pieces(value):
    high = lax.reduce_precision(value, 8, 7)
    rest = value - high
    middle = lax.reduce_precision(rest, 8, 7)
    low = rest - middle
    return [part.astype(jnp.bfloat16) for part in (high, middle, low)]


def normal(values, axes):
    total = jnp.sum(values * values, axis=axes, keepdims=True)
    return (values * lax.rsqrt(total + EPSILON)).astype(jnp.bfloat16)


def spread(value, shape, place):
    lane = lax.broadcasted_iota(jnp.int32, shape, 1) - 3 * place
    lanes = jnp.zeros(shape, jnp.bfloat16)
    for index, part in enumerate(pieces(value)):
        lanes = jnp.where(lane == index, part, lanes)
    return lanes


def from_peer(block, axis, step):
    return lax.ppermute(block, axis, [(at, at ^ step) for at in range(4)])


def in_order(values):
    shape = values.shape
    values = values.reshape(2, 2, 2, 2, -1, shape[1])
    for dim, (axis, bit) in enumerate((("x", 2), ("x", 1), ("zb", 1), ("zh", 1))):
        swap = (lax.axis_index(axis) & bit) != 0
        values = jnp.where(swap, jnp.flip(values, dim), values)
    return values.reshape(shape)


def body(hidden, teacher, projector):
    rows, width = hidden.shape
    full = projector.shape[1]
    group_fs, group_xz = group(FS), group(XZ)
    mine = rows // group_fs
    half = width // 2
    width_t = teacher.shape[1]
    core = lax.axis_index("c")

    partial_embed = dot(hidden, projector).astype(jnp.bfloat16)
    sent = jnp.concatenate(
        [
            partial_embed.reshape(group_fs, mine, full),
            teacher.reshape(group_fs, mine, width_t),
        ],
        axis=2,
    )
    got = exchange(sent, FS)
    embed = jnp.sum(got[:, :, :full].astype(jnp.float32), axis=0)
    inv_student = lax.rsqrt(jnp.sum(embed * embed, axis=1, keepdims=True) + EPSILON)
    unit = embed * inv_student
    student = unit.astype(jnp.bfloat16)
    target = normal(got[:, :, full:].astype(jnp.float32), (0, 2))
    target = target.transpose(1, 0, 2).reshape(mine, -1)

    mine_rows = jnp.concatenate([student, target], axis=1)
    here = gather(jnp.concatenate([student, -target], axis=1), ("y",))
    here = here.reshape(-1, here.shape[2])
    rows_1 = from_peer(mine_rows, STRIDE, 1)
    later, rows_1 = lax.optimization_barrier((mine_rows, rows_1))
    near = [mine_rows, rows_1] + [from_peer(later, STRIDE, step) for step in (2, 3)]
    near, here = lax.optimization_barrier((jnp.concatenate(near, axis=0), here))
    far_1 = from_peer(near, "x", 1)
    there = lax.ppermute(here, "za", SWAP)
    here_core = lax.ppermute(here, "c", SWAP)
    later, here_core = lax.optimization_barrier((near, here_core))
    far = [near, far_1] + [from_peer(later, "x", step) for step in (2, 3)]
    far = lax.optimization_barrier((there, *far))[1:]
    row_block = jnp.concatenate(far, axis=0)
    columns = jnp.concatenate(
        [here, here_core, there, lax.ppermute(there, "c", SWAP)], axis=0
    )
    s_cols = columns[:, :full]
    differ = dot(row_block, columns, ROWS_T)
    differ = in_order(differ)
    squares = jnp.sum(differ * differ)
    squares, hidden_sent = lax.optimization_barrier((squares, hidden))
    squares = squares + lax.ppermute(squares, "c", SWAP)
    hidden_there = lax.ppermute(hidden_sent, "c", SWAP)
    squares, hidden_there = lax.optimization_barrier((squares, hidden_there))
    partial_grad = sum(dot(part, s_cols) for part in pieces(differ)[::-1])
    partial_grad = partial_grad.astype(jnp.bfloat16).reshape(-1, mine, full)
    grad_unit = 4.0 * jnp.sum(exchange(partial_grad, ROW).astype(jnp.float32), axis=0)
    radial = jnp.sum(unit * grad_unit, axis=1, keepdims=True)
    grad_embed = (inv_student * (grad_unit - unit * radial)).astype(jnp.bfloat16)

    wide = gather(
        jnp.concatenate([grad_embed, spread(squares, (mine, 128), lax.axis_index(FS))], axis=1), FS
    ).reshape(rows, -1)
    piece = wide[:, :full]
    piece_there = lax.ppermute(piece, "c", SWAP)
    grad_hidden = dot(piece, projector, ROWS_T)

    left = lax.dynamic_slice_in_dim(hidden, core * half, half, 1)
    left_there = lax.dynamic_slice_in_dim(hidden_there, core * half, half, 1)
    proj_piece = dot(left, piece, COLS_T) + dot(left_there, piece_there, COLS_T)

    loss_row = jnp.sum(
        wide.reshape(group_fs, mine, -1)[:, 0, full:].astype(jnp.float32), axis=0
    )
    loss_row = jnp.pad(loss_row.astype(jnp.bfloat16), (0, full - 128))
    blocks = jnp.concatenate(
        [
            proj_piece.astype(jnp.bfloat16).reshape(group_xz, half // group_xz, full),
            jnp.broadcast_to(loss_row, (group_xz, 1, full)),
        ],
        axis=1,
    )
    summed = jnp.sum(exchange(blocks, XZ).astype(jnp.float32), axis=0)
    loss = jnp.sum(summed[-1]) / (rows * group(DP))
    summed = summed[:-1].astype(jnp.bfloat16)
    grad_proj = lax.all_gather(
        gather(summed, XZ).reshape(half, full), "c", axis=0, tiled=True
    ).astype(jnp.float32)
    return (grad_hidden, grad_proj, loss)


def solution(mesh):
    fine = Mesh(mesh.devices.reshape([SIZES[axis] for axis in DP + FS]), DP + FS)
    return jax.shard_map(
        body,
        mesh=fine,
        in_specs=(P(DP, FS), P(DP, FS), P(FS, None)),
        out_specs=(P(DP, FS), P(FS, None), P()),
        check_vma=False,
    )
```

```python
import jax
import jax.numpy as jnp
from jax import lax
from jax.sharding import Mesh
from jax.sharding import PartitionSpec as P

EPSILON = 1e-06
DP = ("x", "zb", "za", "c")
FS = ("zh", "y")
XZ = ("x", "zb", "za")
STRIDE = ("zb", "za")
ROW = ("x",) + STRIDE
SIZES = {"x": 4, "zb": 2, "za": 2, "c": 2, "zh": 2, "y": 8}
SWAP = [(0, 1), (1, 0)]
ROWS_T = (((1,), (1,)), ((), ()))
COLS_T = (((0,), (0,)), ((), ()))


def dot(a, b, dims=(((1,), (0,)), ((), ()))):
    return lax.dot_general(a, b, dims, preferred_element_type=jnp.float32)


def group(axes):
    total = 1
    for axis in axes:
        total *= SIZES[axis]
    return total


def exchange(blocks, axes):
    return lax.all_to_all(blocks, axes, split_axis=0, concat_axis=0, tiled=True)


def gather(block, axes):
    copies = jnp.broadcast_to(block[None], (group(axes),) + block.shape)
    return exchange(copies, axes)


def pieces(value):
    high = lax.reduce_precision(value, 8, 7)
    rest = value - high
    middle = lax.reduce_precision(rest, 8, 7)
    low = rest - middle
    return [part.astype(jnp.bfloat16) for part in (high, middle, low)]


def normal(values, axes):
    total = jnp.sum(values * values, axis=axes, keepdims=True)
    return (values * lax.rsqrt(total + EPSILON)).astype(jnp.bfloat16)


def spread(value, shape, place):
    lane = lax.broadcasted_iota(jnp.int32, shape, 1) - 3 * place
    lanes = jnp.zeros(shape, jnp.bfloat16)
    for index, part in enumerate(pieces(value)):
        lanes = jnp.where(lane == index, part, lanes)
    return lanes


def around(block, axis):
    blocks = [block]
    for step in (1, 2, 3):
        blocks.append(lax.ppermute(block, axis, [(at, at ^ step) for at in range(4)]))
    return jnp.concatenate(blocks, axis=0)


def in_order(values):
    shape = values.shape
    values = values.reshape(2, 2, 2, 2, -1, shape[1])
    for dim, (axis, bit) in enumerate((("x", 2), ("x", 1), ("zb", 1), ("za", 1))):
        swap = (lax.axis_index(axis) & bit) != 0
        values = jnp.where(swap, jnp.flip(values, dim), values)
    return values.reshape(shape)


def body(hidden, teacher, projector):
    rows, width = hidden.shape
    full = projector.shape[1]
    group_fs, group_xz = group(FS), group(XZ)
    mine = rows // group_fs
    half = width // 2
    width_t = teacher.shape[1]
    core = lax.axis_index("c")

    partial_embed = dot(hidden, projector).astype(jnp.bfloat16)
    sent = jnp.concatenate(
        [
            partial_embed.reshape(group_fs, mine, full),
            teacher.reshape(group_fs, mine, width_t),
        ],
        axis=2,
    )
    got = exchange(sent, FS)
    embed = jnp.sum(got[:, :, :full].astype(jnp.float32), axis=0)
    inv_student = lax.rsqrt(jnp.sum(embed * embed, axis=1, keepdims=True) + EPSILON)
    unit = embed * inv_student
    student = unit.astype(jnp.bfloat16)
    target = normal(got[:, :, full:].astype(jnp.float32), (0, 2))
    target = target.transpose(1, 0, 2).reshape(mine, -1)

    mine_rows, hidden_sent = lax.optimization_barrier(
        (jnp.concatenate([student, target], axis=1), hidden)
    )
    here = gather(jnp.concatenate([student, -target], axis=1), ("y",))
    here = here.reshape(-1, here.shape[2])
    hidden_there = lax.ppermute(hidden_sent, "c", SWAP)
    mine_rows, hidden_there = lax.optimization_barrier((mine_rows, hidden_there))
    row_block = around(around(mine_rows, STRIDE), "x")
    there = lax.ppermute(here, "zh", SWAP)
    columns = jnp.concatenate(
        [here, lax.ppermute(here, "c", SWAP), there, lax.ppermute(there, "c", SWAP)],
        axis=0,
    )
    s_cols = columns[:, :full]
    differ = dot(row_block, columns, ROWS_T)
    differ = in_order(differ)
    squares = jnp.sum(differ * differ)
    squares = squares + lax.ppermute(squares, "c", SWAP)
    partial_grad = sum(dot(part, s_cols) for part in pieces(differ)[::-1])
    partial_grad = partial_grad.astype(jnp.bfloat16).reshape(-1, mine, full)
    grad_unit = 4.0 * jnp.sum(exchange(partial_grad, ROW).astype(jnp.float32), axis=0)
    radial = jnp.sum(unit * grad_unit, axis=1, keepdims=True)
    grad_embed = (inv_student * (grad_unit - unit * radial)).astype(jnp.bfloat16)

    wide = gather(
        jnp.concatenate([grad_embed, spread(squares, (mine, 128), lax.axis_index(FS))], axis=1), FS
    ).reshape(rows, -1)
    piece = wide[:, :full]
    piece_there = lax.ppermute(piece, "c", SWAP)
    grad_hidden = dot(piece, projector, ROWS_T)

    left = lax.dynamic_slice_in_dim(hidden, core * half, half, 1)
    left_there = lax.dynamic_slice_in_dim(hidden_there, core * half, half, 1)
    proj_piece = dot(left, piece, COLS_T) + dot(left_there, piece_there, COLS_T)

    loss_row = jnp.sum(
        wide.reshape(group_fs, mine, -1)[:, 0, full:].astype(jnp.float32), axis=0
    )
    loss_row = jnp.pad(loss_row.astype(jnp.bfloat16), (0, full - 128))
    blocks = jnp.concatenate(
        [
            proj_piece.astype(jnp.bfloat16).reshape(group_xz, half // group_xz, full),
            jnp.broadcast_to(loss_row, (group_xz, 1, full)),
        ],
        axis=1,
    )
    summed = jnp.sum(exchange(blocks, XZ).astype(jnp.float32), axis=0)
    loss = jnp.sum(summed[-1]) / (rows * group(DP))
    summed = summed[:-1].astype(jnp.bfloat16)
    grad_proj = lax.all_gather(
        gather(summed, XZ).reshape(half, full), "c", axis=0, tiled=True
    ).astype(jnp.float32)
    return (grad_hidden, grad_proj, loss)


def solution(mesh):
    fine = Mesh(mesh.devices.reshape([SIZES[axis] for axis in DP + FS]), DP + FS)
    return jax.shard_map(
        body,
        mesh=fine,
        in_specs=(P(DP, FS), P(DP, FS), P(FS, None)),
        out_specs=(P(DP, FS), P(FS, None), P()),
        check_vma=False,
    )
```

```python
import jax
import jax.numpy as jnp
from jax import lax
from jax.sharding import Mesh
from jax.sharding import PartitionSpec as P

EPSILON = 1e-06
DP = ("x", "zb", "za", "c")
FS = ("zh", "y")
XZ = ("x", "zb", "za")
STRIDE = ("zb", "zh")
ROW = ("x",) + STRIDE
SIZES = {"x": 4, "zb": 2, "za": 2, "c": 2, "zh": 2, "y": 8}
SWAP = [(0, 1), (1, 0)]
ROWS_T = (((1,), (1,)), ((), ()))
COLS_T = (((0,), (0,)), ((), ()))


def dot(a, b, dims=(((1,), (0,)), ((), ()))):
    return lax.dot_general(a, b, dims, preferred_element_type=jnp.float32)


def group(axes):
    total = 1
    for axis in axes:
        total *= SIZES[axis]
    return total


def exchange(blocks, axes):
    return lax.all_to_all(blocks, axes, split_axis=0, concat_axis=0, tiled=True)


def gather(block, axes):
    copies = jnp.broadcast_to(block[None], (group(axes),) + block.shape)
    return exchange(copies, axes)


def pieces(value):
    high = lax.reduce_precision(value, 8, 7)
    rest = value - high
    middle = lax.reduce_precision(rest, 8, 7)
    low = rest - middle
    return [part.astype(jnp.bfloat16) for part in (high, middle, low)]


def normal(values, axes):
    total = jnp.sum(values * values, axis=axes, keepdims=True)
    return (values * lax.rsqrt(total + EPSILON)).astype(jnp.bfloat16)


def spread(value, shape, place):
    lane = lax.broadcasted_iota(jnp.int32, shape, 1) - 3 * place
    lanes = jnp.zeros(shape, jnp.bfloat16)
    for index, part in enumerate(pieces(value)):
        lanes = jnp.where(lane == index, part, lanes)
    return lanes


def around(block, axis):
    blocks = [block]
    for step in (1, 2, 3):
        blocks.append(lax.ppermute(block, axis, [(at, at ^ step) for at in range(4)]))
    return jnp.concatenate(blocks, axis=0)


def along_ring(block, other):
    size = SIZES["x"]
    left = [(at, (at + 1) % size) for at in range(size)]
    right = [(at, (at - 1) % size) for at in range(size)]
    after = lax.ppermute(block, "x", right)
    before = lax.ppermute(block, "x", left)
    cut = block.shape[0] // 2
    after, before, other = lax.optimization_barrier((after, before, other))
    upper = lax.ppermute(after[:cut], "x", right)
    lower = lax.ppermute(before[cut:], "x", left)
    return jnp.concatenate([block, after, upper, lower, before], axis=0), other


def in_order(values):
    shape = values.shape
    values = values.reshape(SIZES["x"], 2, 2, -1, shape[1])
    for dim, axis in ((1, "zb"), (2, "zh")):
        values = jnp.where(lax.axis_index(axis) != 0, jnp.flip(values, dim), values)
    for bit in (1, 2):
        swap = (lax.axis_index("x") & bit) != 0
        values = jnp.where(swap, jnp.roll(values, bit, axis=0), values)
    return values.reshape(shape)


def body(hidden, teacher, projector):
    rows, width = hidden.shape
    full = projector.shape[1]
    group_fs, group_xz = group(FS), group(XZ)
    mine = rows // group_fs
    half = width // 2
    width_t = teacher.shape[1]
    core = lax.axis_index("c")

    partial_embed = dot(hidden, projector).astype(jnp.bfloat16)
    sent = jnp.concatenate(
        [
            partial_embed.reshape(group_fs, mine, full),
            teacher.reshape(group_fs, mine, width_t),
        ],
        axis=2,
    )
    got = exchange(sent, FS)
    embed = jnp.sum(got[:, :, :full].astype(jnp.float32), axis=0)
    inv_student = lax.rsqrt(jnp.sum(embed * embed, axis=1, keepdims=True) + EPSILON)
    unit = embed * inv_student
    student = unit.astype(jnp.bfloat16)
    target = normal(got[:, :, full:].astype(jnp.float32), (0, 2))
    target = target.transpose(1, 0, 2).reshape(mine, -1)

    mine_rows, hidden_sent = lax.optimization_barrier(
        (jnp.concatenate([student, target], axis=1), hidden)
    )
    here = gather(jnp.concatenate([student, -target], axis=1), ("y",))
    here = here.reshape(-1, here.shape[2])
    hidden_there = lax.ppermute(hidden_sent, "c", SWAP)
    mine_rows, hidden_there = lax.optimization_barrier((mine_rows, hidden_there))
    there = lax.ppermute(here, "za", SWAP)
    row_block, _ = along_ring(around(mine_rows, STRIDE), here)
    columns = jnp.concatenate(
        [here, lax.ppermute(here, "c", SWAP), there, lax.ppermute(there, "c", SWAP)],
        axis=0,
    )
    s_cols = columns[:, :full]
    differ = dot(row_block, columns, ROWS_T)
    differ = in_order(differ)
    squares = jnp.sum(differ * differ)
    squares = squares + lax.ppermute(squares, "c", SWAP)
    partial_grad = sum(dot(part, s_cols) for part in pieces(differ)[::-1])
    partial_grad = partial_grad.astype(jnp.bfloat16).reshape(-1, mine, full)
    grad_unit = 4.0 * jnp.sum(exchange(partial_grad, ROW).astype(jnp.float32), axis=0)
    radial = jnp.sum(unit * grad_unit, axis=1, keepdims=True)
    grad_embed = (inv_student * (grad_unit - unit * radial)).astype(jnp.bfloat16)

    wide = gather(
        jnp.concatenate([grad_embed, spread(squares, (mine, 128), lax.axis_index(FS))], axis=1), FS
    ).reshape(rows, -1)
    piece = wide[:, :full]
    piece_there = lax.ppermute(piece, "c", SWAP)
    grad_hidden = dot(piece, projector, ROWS_T)

    left = lax.dynamic_slice_in_dim(hidden, core * half, half, 1)
    left_there = lax.dynamic_slice_in_dim(hidden_there, core * half, half, 1)
    proj_piece = dot(left, piece, COLS_T) + dot(left_there, piece_there, COLS_T)

    loss_row = jnp.sum(
        wide.reshape(group_fs, mine, -1)[:, 0, full:].astype(jnp.float32), axis=0
    )
    loss_row = jnp.pad(loss_row.astype(jnp.bfloat16), (0, full - 128))
    blocks = jnp.concatenate(
        [
            proj_piece.astype(jnp.bfloat16).reshape(group_xz, half // group_xz, full),
            jnp.broadcast_to(loss_row, (group_xz, 1, full)),
        ],
        axis=1,
    )
    summed = jnp.sum(exchange(blocks, XZ).astype(jnp.float32), axis=0)
    loss = jnp.sum(summed[-1]) / (rows * group(DP))
    summed = summed[:-1].astype(jnp.bfloat16)
    grad_proj = lax.all_gather(
        gather(summed, XZ).reshape(half, full), "c", axis=0, tiled=True
    ).astype(jnp.float32)
    return (grad_hidden, grad_proj, loss)


def solution(mesh):
    fine = Mesh(mesh.devices.reshape([SIZES[axis] for axis in DP + FS]), DP + FS)
    return jax.shard_map(
        body,
        mesh=fine,
        in_specs=(P(DP, FS), P(DP, FS), P(FS, None)),
        out_specs=(P(DP, FS), P(FS, None), P()),
        check_vma=False,
    )
```

```python
import jax
import jax.numpy as jnp
from jax import lax
from jax.sharding import Mesh
from jax.sharding import PartitionSpec as P

EPSILON = 1e-06
DP = ("x", "zb", "za", "c")
FS = ("zh", "y")
XZ = ("x", "zb", "za")
STRIDE = ("zb", "zh")
ROW = ("x",) + STRIDE
SIZES = {"x": 4, "zb": 2, "za": 2, "c": 2, "zh": 2, "y": 8}
SWAP = [(0, 1), (1, 0)]
ROWS_T = (((1,), (1,)), ((), ()))
COLS_T = (((0,), (0,)), ((), ()))


def dot(a, b, dims=(((1,), (0,)), ((), ()))):
    return lax.dot_general(a, b, dims, preferred_element_type=jnp.float32)


def group(axes):
    total = 1
    for axis in axes:
        total *= SIZES[axis]
    return total


def exchange(blocks, axes):
    return lax.all_to_all(blocks, axes, split_axis=0, concat_axis=0, tiled=True)


def gather(block, axes):
    copies = jnp.broadcast_to(block[None], (group(axes),) + block.shape)
    return exchange(copies, axes)


def pieces(value):
    high = lax.reduce_precision(value, 8, 7)
    rest = value - high
    middle = lax.reduce_precision(rest, 8, 7)
    low = rest - middle
    return [part.astype(jnp.bfloat16) for part in (high, middle, low)]


def normal(values, axes):
    total = jnp.sum(values * values, axis=axes, keepdims=True)
    return (values * lax.rsqrt(total + EPSILON)).astype(jnp.bfloat16)


def spread(value, shape, place):
    lane = lax.broadcasted_iota(jnp.int32, shape, 1) - 3 * place
    lanes = jnp.zeros(shape, jnp.bfloat16)
    for index, part in enumerate(pieces(value)):
        lanes = jnp.where(lane == index, part, lanes)
    return lanes


def from_peer(block, axis, step):
    return lax.ppermute(block, axis, [(at, at ^ step) for at in range(4)])


def in_order(values):
    shape = values.shape
    values = values.reshape(2, 2, 2, 2, -1, shape[1])
    for dim, (axis, bit) in enumerate((("x", 2), ("x", 1), ("zb", 1), ("zh", 1))):
        swap = (lax.axis_index(axis) & bit) != 0
        values = jnp.where(swap, jnp.flip(values, dim), values)
    return values.reshape(shape)


def body(hidden, teacher, projector):
    rows, width = hidden.shape
    full = projector.shape[1]
    group_fs, group_xz = group(FS), group(XZ)
    mine = rows // group_fs
    half = width // 2
    width_t = teacher.shape[1]
    core = lax.axis_index("c")

    partial_embed = dot(hidden, projector).astype(jnp.bfloat16)
    sent = jnp.concatenate(
        [
            partial_embed.reshape(group_fs, mine, full),
            teacher.reshape(group_fs, mine, width_t),
        ],
        axis=2,
    )
    got = exchange(sent, FS)
    embed = jnp.sum(got[:, :, :full].astype(jnp.float32), axis=0)
    inv_student = lax.rsqrt(jnp.sum(embed * embed, axis=1, keepdims=True) + EPSILON)
    unit = embed * inv_student
    student = unit.astype(jnp.bfloat16)
    target = normal(got[:, :, full:].astype(jnp.float32), (0, 2))
    target = target.transpose(1, 0, 2).reshape(mine, -1)

    mine_rows, hidden_sent = lax.optimization_barrier(
        (jnp.concatenate([student, target], axis=1), hidden)
    )
    here = gather(jnp.concatenate([student, -target], axis=1), ("y",))
    here = here.reshape(-1, here.shape[2])
    hidden_there = lax.ppermute(hidden_sent, "c", SWAP)
    mine_rows, hidden_there = lax.optimization_barrier((mine_rows, hidden_there))
    near = [mine_rows] + [from_peer(mine_rows, STRIDE, step) for step in (1, 2, 3)]
    near = jnp.concatenate(near, axis=0)
    _, here = lax.optimization_barrier((near, here))
    far_1 = from_peer(near, "x", 1)
    there = lax.ppermute(here, "za", SWAP)
    here_core = lax.ppermute(here, "c", SWAP)
    far = [near, far_1] + [from_peer(near, "x", step) for step in (2, 3)]
    far = lax.optimization_barrier((there, *far))[1:]
    row_block = jnp.concatenate(far, axis=0)
    columns = jnp.concatenate(
        [here, here_core, there, lax.ppermute(there, "c", SWAP)], axis=0
    )
    s_cols = columns[:, :full]
    differ = dot(row_block, columns, ROWS_T)
    differ = in_order(differ)
    squares = jnp.sum(differ * differ)
    squares = squares + lax.ppermute(squares, "c", SWAP)
    partial_grad = sum(dot(part, s_cols) for part in pieces(differ)[::-1])
    partial_grad = partial_grad.astype(jnp.bfloat16).reshape(-1, mine, full)
    grad_unit = 4.0 * jnp.sum(exchange(partial_grad, ROW).astype(jnp.float32), axis=0)
    radial = jnp.sum(unit * grad_unit, axis=1, keepdims=True)
    grad_embed = (inv_student * (grad_unit - unit * radial)).astype(jnp.bfloat16)

    wide = gather(
        jnp.concatenate([grad_embed, spread(squares, (mine, 128), lax.axis_index(FS))], axis=1), FS
    ).reshape(rows, -1)
    piece = wide[:, :full]
    piece_there = lax.ppermute(piece, "c", SWAP)
    grad_hidden = dot(piece, projector, ROWS_T)

    left = lax.dynamic_slice_in_dim(hidden, core * half, half, 1)
    left_there = lax.dynamic_slice_in_dim(hidden_there, core * half, half, 1)
    proj_piece = dot(left, piece, COLS_T) + dot(left_there, piece_there, COLS_T)

    loss_row = jnp.sum(
        wide.reshape(group_fs, mine, -1)[:, 0, full:].astype(jnp.float32), axis=0
    )
    loss_row = jnp.pad(loss_row.astype(jnp.bfloat16), (0, full - 128))
    blocks = jnp.concatenate(
        [
            proj_piece.astype(jnp.bfloat16).reshape(group_xz, half // group_xz, full),
            jnp.broadcast_to(loss_row, (group_xz, 1, full)),
        ],
        axis=1,
    )
    summed = jnp.sum(exchange(blocks, XZ).astype(jnp.float32), axis=0)
    loss = jnp.sum(summed[-1]) / (rows * group(DP))
    summed = summed[:-1].astype(jnp.bfloat16)
    grad_proj = lax.all_gather(
        gather(summed, XZ).reshape(half, full), "c", axis=0, tiled=True
    ).astype(jnp.float32)
    return (grad_hidden, grad_proj, loss)


def solution(mesh):
    fine = Mesh(mesh.devices.reshape([SIZES[axis] for axis in DP + FS]), DP + FS)
    return jax.shard_map(
        body,
        mesh=fine,
        in_specs=(P(DP, FS), P(DP, FS), P(FS, None)),
        out_specs=(P(DP, FS), P(FS, None), P()),
        check_vma=False,
    )
```

```python
import jax
import jax.numpy as jnp
from jax import lax
from jax.sharding import Mesh
from jax.sharding import PartitionSpec as P

EPSILON = 1e-06
DP = ("x", "zb", "za", "c")
FS = ("zh", "y")
XZ = ("x", "zb", "za")
STRIDE = ("zb", "zh")
ROW = ("x",) + STRIDE
SIZES = {"x": 4, "zb": 2, "za": 2, "c": 2, "zh": 2, "y": 8}
SWAP = [(0, 1), (1, 0)]
ROWS_T = (((1,), (1,)), ((), ()))
COLS_T = (((0,), (0,)), ((), ()))


def dot(a, b, dims=(((1,), (0,)), ((), ()))):
    return lax.dot_general(a, b, dims, preferred_element_type=jnp.float32)


def group(axes):
    total = 1
    for axis in axes:
        total *= SIZES[axis]
    return total


def exchange(blocks, axes):
    return lax.all_to_all(blocks, axes, split_axis=0, concat_axis=0, tiled=True)


def gather(block, axes):
    copies = jnp.broadcast_to(block[None], (group(axes),) + block.shape)
    return exchange(copies, axes)


def pieces(value):
    high = lax.reduce_precision(value, 8, 7)
    rest = value - high
    middle = lax.reduce_precision(rest, 8, 7)
    low = rest - middle
    return [part.astype(jnp.bfloat16) for part in (high, middle, low)]


def normal(values, axes):
    total = jnp.sum(values * values, axis=axes, keepdims=True)
    return (values * lax.rsqrt(total + EPSILON)).astype(jnp.bfloat16)


def spread(value, shape, place):
    lane = lax.broadcasted_iota(jnp.int32, shape, 1) - 3 * place
    lanes = jnp.zeros(shape, jnp.bfloat16)
    for index, part in enumerate(pieces(value)):
        lanes = jnp.where(lane == index, part, lanes)
    return lanes


def around(block, axis):
    blocks = [block]
    for step in (1, 2, 3):
        blocks.append(lax.ppermute(block, axis, [(at, at ^ step) for at in range(4)]))
    return jnp.concatenate(blocks, axis=0)


def in_order(values):
    shape = values.shape
    values = values.reshape(2, 2, 2, 2, -1, shape[1])
    for dim, (axis, bit) in enumerate((("x", 2), ("x", 1), ("zb", 1), ("zh", 1))):
        swap = (lax.axis_index(axis) & bit) != 0
        values = jnp.where(swap, jnp.flip(values, dim), values)
    return values.reshape(shape)


def body(hidden, teacher, projector):
    rows, width = hidden.shape
    full = projector.shape[1]
    group_fs, group_xz = group(FS), group(XZ)
    mine = rows // group_fs
    half = width // 2
    width_t = teacher.shape[1]
    core = lax.axis_index("c")

    partial_embed = dot(hidden, projector).astype(jnp.bfloat16)
    sent = jnp.concatenate(
        [
            partial_embed.reshape(group_fs, mine, full),
            teacher.reshape(group_fs, mine, width_t),
        ],
        axis=2,
    )
    got = exchange(sent, FS)
    embed = jnp.sum(got[:, :, :full].astype(jnp.float32), axis=0)
    inv_student = lax.rsqrt(jnp.sum(embed * embed, axis=1, keepdims=True) + EPSILON)
    unit = embed * inv_student
    student = unit.astype(jnp.bfloat16)
    target = normal(got[:, :, full:].astype(jnp.float32), (0, 2))
    target = target.transpose(1, 0, 2).reshape(mine, -1)

    mine_rows, hidden_sent = lax.optimization_barrier(
        (jnp.concatenate([student, target], axis=1), hidden)
    )
    here = gather(jnp.concatenate([student, -target], axis=1), ("y",))
    here = here.reshape(-1, here.shape[2])
    hidden_there = lax.ppermute(hidden_sent, "c", SWAP)
    mine_rows, hidden_there = lax.optimization_barrier((mine_rows, hidden_there))
    row_block = around(around(mine_rows, STRIDE), "x")
    there = lax.ppermute(here, "za", SWAP)
    columns = jnp.concatenate(
        [here, lax.ppermute(here, "c", SWAP), there, lax.ppermute(there, "c", SWAP)],
        axis=0,
    )
    s_cols = columns[:, :full]
    differ = dot(row_block, columns, ROWS_T)
    differ = in_order(differ)
    squares = jnp.sum(differ * differ)
    squares = squares + lax.ppermute(squares, "c", SWAP)
    partial_grad = sum(dot(part, s_cols) for part in pieces(differ)[::-1])
    partial_grad = partial_grad.astype(jnp.bfloat16).reshape(-1, mine, full)
    grad_unit = 4.0 * jnp.sum(exchange(partial_grad, ROW).astype(jnp.float32), axis=0)
    radial = jnp.sum(unit * grad_unit, axis=1, keepdims=True)
    grad_embed = (inv_student * (grad_unit - unit * radial)).astype(jnp.bfloat16)

    wide = gather(
        jnp.concatenate([grad_embed, spread(squares, (mine, 128), lax.axis_index(FS))], axis=1), FS
    ).reshape(rows, -1)
    piece = wide[:, :full]
    piece_there = lax.ppermute(piece, "c", SWAP)
    grad_hidden = dot(piece, projector, ROWS_T)

    left = lax.dynamic_slice_in_dim(hidden, core * half, half, 1)
    left_there = lax.dynamic_slice_in_dim(hidden_there, core * half, half, 1)
    proj_piece = dot(
        jnp.concatenate([left, left_there], axis=0),
        jnp.concatenate([piece, piece_there], axis=0),
        COLS_T,
    )

    loss_row = jnp.sum(
        wide.reshape(group_fs, mine, -1)[:, 0, full:].astype(jnp.float32), axis=0
    )
    loss_row = jnp.pad(loss_row.astype(jnp.bfloat16), (0, full - 128))
    blocks = jnp.concatenate(
        [
            proj_piece.astype(jnp.bfloat16).reshape(group_xz, half // group_xz, full),
            jnp.broadcast_to(loss_row, (group_xz, 1, full)),
        ],
        axis=1,
    )
    summed = jnp.sum(exchange(blocks, XZ).astype(jnp.float32), axis=0)
    loss = jnp.sum(summed[-1]) / (rows * group(DP))
    summed = summed[:-1].astype(jnp.bfloat16)
    grad_proj = lax.all_gather(
        gather(summed, XZ).reshape(half, full), "c", axis=0, tiled=True
    ).astype(jnp.float32)
    return (grad_hidden, grad_proj, loss)


def solution(mesh):
    fine = Mesh(mesh.devices.reshape([SIZES[axis] for axis in DP + FS]), DP + FS)
    return jax.shard_map(
        body,
        mesh=fine,
        in_specs=(P(DP, FS), P(DP, FS), P(FS, None)),
        out_specs=(P(DP, FS), P(FS, None), P()),
        check_vma=False,
    )
```

```python
import jax
import jax.numpy as jnp
from jax import lax
from jax.sharding import Mesh
from jax.sharding import PartitionSpec as P

EPSILON = 1e-06
DP = ("x", "zb", "za", "c")
FS = ("zh", "y")
XZ = ("x", "zb", "za")
STRIDE = ("zb", "zh")
ROW = ("x",) + STRIDE
SIZES = {"x": 4, "zb": 2, "za": 2, "c": 2, "zh": 2, "y": 8}
SWAP = [(0, 1), (1, 0)]
ROWS_T = (((1,), (1,)), ((), ()))
COLS_T = (((0,), (0,)), ((), ()))


def dot(a, b, dims=(((1,), (0,)), ((), ()))):
    return lax.dot_general(a, b, dims, preferred_element_type=jnp.float32)


def group(axes):
    total = 1
    for axis in axes:
        total *= SIZES[axis]
    return total


def exchange(blocks, axes):
    return lax.all_to_all(blocks, axes, split_axis=0, concat_axis=0, tiled=True)


def gather(block, axes):
    copies = jnp.broadcast_to(block[None], (group(axes),) + block.shape)
    return exchange(copies, axes)


def pieces(value):
    high = lax.reduce_precision(value, 8, 7)
    rest = value - high
    middle = lax.reduce_precision(rest, 8, 7)
    low = rest - middle
    return [part.astype(jnp.bfloat16) for part in (high, middle, low)]


def normal(values, axes):
    total = jnp.sum(values * values, axis=axes, keepdims=True)
    return (values * lax.rsqrt(total + EPSILON)).astype(jnp.bfloat16)


def spread(value, shape, place):
    lane = lax.broadcasted_iota(jnp.int32, shape, 1) - 3 * place
    lanes = jnp.zeros(shape, jnp.bfloat16)
    for index, part in enumerate(pieces(value)):
        lanes = jnp.where(lane == index, part, lanes)
    return lanes


def around(block, axis):
    blocks = [block]
    for step in (1, 2, 3):
        blocks.append(lax.ppermute(block, axis, [(at, at ^ step) for at in range(4)]))
    return jnp.concatenate(blocks, axis=0)


def along_ring(block, other):
    size = SIZES["x"]
    left = [(at, (at + 1) % size) for at in range(size)]
    right = [(at, (at - 1) % size) for at in range(size)]
    after = lax.ppermute(block, "x", right)
    before = lax.ppermute(block, "x", left)
    cut = block.shape[0] // 2
    after, before, other = lax.optimization_barrier((after, before, other))
    upper = lax.ppermute(after[:cut], "x", right)
    lower = lax.ppermute(before[cut:], "x", left)
    return jnp.concatenate([block, after, upper, lower, before], axis=0), other


def in_order(values):
    shape = values.shape
    values = values.reshape(SIZES["x"], 2, 2, -1, shape[1])
    for dim, axis in ((1, "zb"), (2, "zh")):
        values = jnp.where(lax.axis_index(axis) != 0, jnp.flip(values, dim), values)
    for bit in (1, 2):
        swap = (lax.axis_index("x") & bit) != 0
        values = jnp.where(swap, jnp.roll(values, bit, axis=0), values)
    return values.reshape(shape)


def body(hidden, teacher, projector):
    rows, width = hidden.shape
    full = projector.shape[1]
    group_fs, group_xz = group(FS), group(XZ)
    mine = rows // group_fs
    half = width // 2
    width_t = teacher.shape[1]
    core = lax.axis_index("c")

    partial_embed = dot(hidden, projector).astype(jnp.bfloat16)
    sent = jnp.concatenate(
        [
            partial_embed.reshape(group_fs, mine, full),
            teacher.reshape(group_fs, mine, width_t),
        ],
        axis=2,
    )
    got = exchange(sent, FS)
    embed = jnp.sum(got[:, :, :full].astype(jnp.float32), axis=0)
    inv_student = lax.rsqrt(jnp.sum(embed * embed, axis=1, keepdims=True) + EPSILON)
    unit = embed * inv_student
    student = unit.astype(jnp.bfloat16)
    target = normal(got[:, :, full:].astype(jnp.float32), (0, 2))
    target = target.transpose(1, 0, 2).reshape(mine, -1)

    mine_rows, hidden_sent = lax.optimization_barrier(
        (jnp.concatenate([student, target], axis=1), hidden)
    )
    here = gather(jnp.concatenate([student, -target], axis=1), ("y",))
    here = here.reshape(-1, here.shape[2])
    hidden_there = lax.ppermute(hidden_sent, "c", SWAP)
    mine_rows, hidden_there = lax.optimization_barrier((mine_rows, hidden_there))
    there = lax.ppermute(here, "za", SWAP)
    row_block, _ = along_ring(around(mine_rows, STRIDE), here)
    columns = jnp.concatenate(
        [here, lax.ppermute(here, "c", SWAP), there, lax.ppermute(there, "c", SWAP)],
        axis=0,
    )
    s_cols = columns[:, :full]
    differ = dot(row_block, columns, ROWS_T)
    differ = in_order(differ)
    squares = jnp.sum(differ * differ)
    squares = squares + lax.ppermute(squares, "c", SWAP)
    partial_grad = sum(dot(part, s_cols) for part in pieces(differ)[::-1])
    partial_grad = partial_grad.astype(jnp.bfloat16).reshape(-1, mine, full)
    grad_unit = 4.0 * jnp.sum(exchange(partial_grad, ROW).astype(jnp.float32), axis=0)
    radial = jnp.sum(unit * grad_unit, axis=1, keepdims=True)
    grad_embed = (inv_student * (grad_unit - unit * radial)).astype(jnp.bfloat16)

    wide = gather(
        jnp.concatenate([grad_embed, spread(squares, (mine, 128), lax.axis_index(FS))], axis=1), FS
    ).reshape(rows, -1)
    piece = wide[:, :full]
    piece_there = lax.ppermute(piece, "c", SWAP)
    grad_hidden = dot(piece, projector, ROWS_T)

    left = lax.dynamic_slice_in_dim(hidden, core * half, half, 1)
    left_there = lax.dynamic_slice_in_dim(hidden_there, core * half, half, 1)
    proj_piece = dot(
        jnp.concatenate([left, left_there], axis=0),
        jnp.concatenate([piece, piece_there], axis=0),
        COLS_T,
    )

    loss_row = jnp.sum(
        wide.reshape(group_fs, mine, -1)[:, 0, full:].astype(jnp.float32), axis=0
    )
    loss_row = jnp.pad(loss_row.astype(jnp.bfloat16), (0, full - 128))
    blocks = jnp.concatenate(
        [
            proj_piece.astype(jnp.bfloat16).reshape(group_xz, half // group_xz, full),
            jnp.broadcast_to(loss_row, (group_xz, 1, full)),
        ],
        axis=1,
    )
    summed = jnp.sum(exchange(blocks, XZ).astype(jnp.float32), axis=0)
    loss = jnp.sum(summed[-1]) / (rows * group(DP))
    summed = summed[:-1].astype(jnp.bfloat16)
    grad_proj = lax.all_gather(
        gather(summed, XZ).reshape(half, full), "c", axis=0, tiled=True
    ).astype(jnp.float32)
    return (grad_hidden, grad_proj, loss)


def solution(mesh):
    fine = Mesh(mesh.devices.reshape([SIZES[axis] for axis in DP + FS]), DP + FS)
    return jax.shard_map(
        body,
        mesh=fine,
        in_specs=(P(DP, FS), P(DP, FS), P(FS, None)),
        out_specs=(P(DP, FS), P(FS, None), P()),
        check_vma=False,
    )
```
